512 devices in a mesh: dp: 16 (over y, x), fsdp: 32 (over z, core).
Axes of the slice: x: 4, y: 4, z: 16, core: 2. Of those that a mesh axis runs over, the one named last changes fastest.
Arguments:
- projections: bfloat16 [65536, 3, 2048], P(('dp', 'fsdp')), parts along dimension 0, may hold values from -6 to 6
- positions: int32 [3, 65536], P(None, ('dp', 'fsdp')), parts along dimension 1, may hold values from 0 to 63
- packed_index: int32 [65536], P(('dp', 'fsdp')), parts along dimension 0, may hold values from 0 to 4095, as said below
- clip_length: int32 [384], P('dp'), parts along dimension 0, may hold values from 64 to 832, as said below
- clip_group: int32 [384], P('dp'), parts along dimension 0, may hold values from 0 to 5, as said below
- query_gain: float32 [128], replicated, may hold values from 0.5 to 1.5
- key_gain: float32 [128], replicated, may hold values from 0.5 to 1.5
- out_weight: bfloat16 [2048, 1536], P('fsdp'), may hold values from -1 to 1
Outputs:
- mixed_rows: bfloat16 [65536, 1536], P(('dp', 'fsdp')), parts along dimension 0
The draws below stay inside these ranges and needn't reach their ends.
There are 16 independent parts, one for each index of `dp`. The reference program is written for one: setup_inputs(seed, part) draws one part's arguments, and reference() takes and returns one part's arrays. A program takes and returns all parts, laid end to end along the dimension named above; an argument that names none is the same for every part. Nothing has to cross between parts.
Inputs may be any that keep to these rules, and one draw needn't show every extreme that they name: `packed_index`: A permutation of the packed positions; the 128 rows of each aligned block send exactly 4 rows to each aligned block of 128 packed positions. `clip_group`: each sequence group is named by exactly 4 clips. `clip_length`: the clips of a group add up to that group's packed positions.
All inputs are finite; a program needn't handle non-finite values.
Results may differ from the reference program's by a relative error of at most 0.0071.
Values may be sent and summed in bfloat16 or wider, within the bound.
A program may use at most 64 MiB of HBM per device.

```python
import math
import jax
import jax.numpy as jnp
import numpy as np
from jax import lax

HEADS = 16
HD = 128
DOUT = 1536
TOK_DEV = 128
CPG = 4
TOKENS = 4096
GBIG = 8
NBIG = 2
NGROUPS = 6
NCLIPS = 24
N_FSDP = 32


def clip_plan(key):
    cut_key, slot_key, order_key = jax.random.split(key, 3)
    group_ids = jnp.arange(NGROUPS, dtype=jnp.int32)
    capacity = jnp.where(group_ids < NBIG, GBIG * TOK_DEV, 4 * TOK_DEV).astype(jnp.int32)
    margin = TOK_DEV // 2
    extra = capacity - CPG * margin
    raw_cuts = jax.random.randint(cut_key, (NGROUPS, CPG - 1), 0, 1 << 20, dtype=jnp.int32)
    cuts = jnp.sort(raw_cuts % (extra[:, None] + 1), axis=1)
    edges = jnp.concatenate([jnp.zeros((NGROUPS, 1), jnp.int32), cuts, extra[:, None]], axis=1)
    inner = margin + edges[:, 1:] - edges[:, :-1]
    big_slot = jax.random.randint(slot_key, (), 0, CPG, dtype=jnp.int32)
    slot_ids = jnp.arange(CPG, dtype=jnp.int32)
    first_row = jnp.where(slot_ids == big_slot, margin + extra[0], margin).astype(jnp.int32)
    inner = inner.at[0].set(first_row)
    shuffled = jax.random.permutation(order_key, NCLIPS).astype(jnp.int32)
    group_of_clip = shuffled // CPG
    clip_ids = jnp.arange(NCLIPS, dtype=jnp.int32)
    before = (group_of_clip[None, :] == group_of_clip[:, None]) & (clip_ids[None, :] < clip_ids[:, None])
    rank = jnp.sum(before.astype(jnp.int32), axis=1)
    lengths = inner[group_of_clip, rank]
    return (lengths.astype(jnp.int32), group_of_clip)


def draw_clip_length(key, part):
    plan = clip_plan(key)
    return plan[0]


def draw_clip_group(key, part):
    plan = clip_plan(key)
    return plan[1]


def draw_packed_index(key, part):
    key = jax.random.fold_in(key, 7)
    peer_rows = TOK_DEV // N_FSDP
    source_key, target_key = jax.random.split(key)
    source_perm = jax.vmap(lambda sub_key: jax.random.permutation(sub_key, TOK_DEV))(jax.random.split(source_key, N_FSDP)).astype(jnp.int32)
    target_perm = jax.vmap(lambda sub_key: jax.random.permutation(sub_key, TOK_DEV))(jax.random.split(target_key, N_FSDP)).astype(jnp.int32)
    send_ids = jnp.arange(TOK_DEV, dtype=jnp.int32)
    target = send_ids // peer_rows
    within = send_ids % peer_rows
    sources = jnp.arange(N_FSDP, dtype=jnp.int32)[:, None]
    entries = target[None, :] * TOK_DEV + target_perm[target[None, :], sources * peer_rows + within[None, :]]
    result = jnp.zeros((N_FSDP, TOK_DEV), jnp.int32).at[sources, source_perm].set(entries)
    return result.reshape(TOKENS)


def place_ends(values, key, least, largest):
    spot = [jax.random.randint(jax.random.fold_in(key, axis), (), 0, length) for axis, length in enumerate(values.shape)]
    main_axis = values.shape.index(max(values.shape))
    next_to = spot[:main_axis] + [(spot[main_axis] + 1) % values.shape[main_axis]] + spot[main_axis + 1:]
    return values.at[tuple(spot)].set(least).at[tuple(next_to)].set(largest)


def steps_of(own_key, shape, cuts, smallest, top_value):
    level = 1.0
    for axis_at, parts in cuts:
        heights = jax.random.uniform(jax.random.fold_in(jax.random.fold_in(own_key, 6), axis_at), (parts,), jnp.float32, smallest / len(cuts), top_value / len(cuts))
        level = level * jnp.repeat(jnp.exp(heights), shape[axis_at] // parts).reshape((-1,) + (1,) * (len(shape) - 1 - axis_at))
    return level


def centred(key, extent, scale, limit, shards=(), held_as=jnp.bfloat16):
    drawn = scale * jax.random.normal(key, extent, jnp.float32)
    if shards:
        drawn = drawn * steps_of(key, extent, shards, -0.22, 0.18)
    return jnp.clip(drawn, -limit, limit).astype(held_as)


def setup_inputs(seed: int = 0, part: int = 0) -> dict:
    arg_keys = jax.random.split(jax.random.key(seed), 9)
    part_keys = jax.random.split(jax.random.fold_in(arg_keys[8], part), 9)
    return {
        "projections": centred(part_keys[0], (TOKENS, 3, HEADS * HD), 1.0, 6.0, ((0, 32),)),
        "positions": place_ends(jax.random.randint(part_keys[1], (3, TOKENS), 0, 64), jax.random.fold_in(part_keys[1], 1), 0, 63).astype(jnp.int32),
        "packed_index": draw_packed_index(jax.random.fold_in(jax.random.fold_in(arg_keys[8], part), 71), part),
        "clip_length": draw_clip_length(jax.random.fold_in(jax.random.fold_in(arg_keys[8], part), 71), part),
        "clip_group": draw_clip_group(jax.random.fold_in(jax.random.fold_in(arg_keys[8], part), 71), part),
        "query_gain": jnp.clip(1.0 + 0.1 * jax.random.normal(arg_keys[5], (HD,), jnp.float32), 0.5, 1.5),
        "key_gain": jnp.clip(1.0 + 0.1 * jax.random.normal(arg_keys[6], (HD,), jnp.float32), 0.5, 1.5),
        "out_weight": centred(arg_keys[7], (HEADS * HD, DOUT), (HEADS * HD // 64) ** -0.5, 1.0, ((0, 32),)),
    }


ROPE_BASE = 256.0
NORM_EPS = 1e-06

def rope_tables(head_width):
    lead_width = head_width // 8
    side_width = (head_width - lead_width) // 2
    axis_list, freq_list, partner_list, sign_list = ([], [], [], [])
    offset = 0
    for axis_number, section in enumerate([lead_width, side_width, side_width]):
        middle = section // 2
        for column in range(section):
            within = column % middle
            axis_list.append(axis_number)
            freq_list.append(ROPE_BASE ** (-2.0 * within / section))
            if column < middle:
                partner_list.append(offset + column + middle)
                sign_list.append(-1.0)
            else:
                partner_list.append(offset + column - middle)
                sign_list.append(1.0)
        offset += section
    return (np.array(axis_list, np.int32), np.array(freq_list, np.float32), np.array(partner_list, np.int32), np.array(sign_list, np.float32))

def rotate_heads(projections, positions, query_gain, key_gain):
    row_count = projections.shape[0]
    head_count = projections.shape[2] // HD
    axis_table, freq_table, partner_table, sign_table = rope_tables(HD)
    angles = positions.astype(jnp.float32)[axis_table, :].T * freq_table[None, :]
    cosine = jnp.cos(angles)[:, None, :]
    sine_part = jnp.sin(angles)[:, None, :]

    def normed(entries, gain):
        entries = entries.astype(jnp.float32).reshape(row_count, head_count, HD)
        factor = lax.rsqrt(lax.optimization_barrier(jnp.mean(entries * entries, axis=-1, keepdims=True)) + NORM_EPS)
        entries = entries * factor * gain
        turned = entries * cosine + entries[..., partner_table] * sign_table * sine_part
        return turned.reshape(row_count, head_count * HD).astype(jnp.bfloat16)
    return (normed(projections[:, 0], query_gain), normed(projections[:, 1], key_gain))

def clip_ends(group_id, clip_length, clip_group):
    count = clip_length.shape[0]
    clip_ids = jnp.arange(count, dtype=jnp.int32)
    inside = clip_group == group_id
    earlier = inside[None, :] & (clip_ids[None, :] <= clip_ids[:, None])
    ends = lax.optimization_barrier(jnp.sum(jnp.where(earlier, clip_length[None, :], 0), axis=1)).astype(jnp.int32)
    return jnp.where(inside, ends, jnp.int32(1 << 30)).astype(jnp.int32)

def clip_labels(spots, ends):
    return lax.optimization_barrier(jnp.sum((spots[:, None] >= ends[None, :]).astype(jnp.int32), axis=1)).astype(jnp.int32)

def reference(projections, positions, packed_index, clip_length, clip_group, query_gain, key_gain, out_weight):
    rotated_query, rotated_key = rotate_heads(projections, positions, query_gain, key_gain)
    inverse = jnp.argsort(packed_index)
    packed_query = rotated_query[inverse]
    packed_key = rotated_key[inverse]
    packed_value = projections[:, 2][inverse]
    halfway = N_FSDP // 2
    big_size = min(8, halfway)
    score_scale = 1.0 / math.sqrt(HD)
    outputs = []
    group_first = 0
    for group_number in range(NGROUPS):
        group_rows = (big_size if group_number < NBIG else 4) * TOK_DEV
        ends = clip_ends(group_number, clip_length, clip_group)
        labels = clip_labels(jnp.arange(group_rows, dtype=jnp.int32), ends)
        allowed = labels[:, None] == labels[None, :]

        def heads_of(source):
            block = source[group_first:group_first + group_rows]
            return block.reshape(group_rows, HEADS, HD).transpose(1, 0, 2)

        def one_head(triple):
            query_head, key_head, value_head = triple
            scores = jnp.dot(query_head, key_head.T, preferred_element_type=jnp.float32) * score_scale
            weights = jnp.where(allowed, jnp.exp(scores), 0.0)
            weights = (weights / lax.optimization_barrier(jnp.sum(weights, axis=-1, keepdims=True))).astype(jnp.bfloat16)
            return jnp.dot(weights, value_head, preferred_element_type=jnp.float32).astype(jnp.bfloat16)
        result = lax.map(one_head, (heads_of(packed_query), heads_of(packed_key), heads_of(packed_value)))
        outputs.append(result.transpose(1, 0, 2).reshape(group_rows, HEADS * HD))
        group_first += group_rows
    attended = jnp.concatenate(outputs, axis=0)
    mixed_packed = jnp.dot(attended, out_weight, preferred_element_type=jnp.float32).astype(jnp.bfloat16)
    return mixed_packed[packed_index]
```

```python
import functools
import math

import jax
import jax.numpy as jnp
import numpy as np
from jax import lax
from jax.experimental import pallas as pl
from jax.experimental.pallas import tpu as pltpu
from jax.sharding import PartitionSpec as P

MESH = pl.DeviceIdType.MESH
HD = 128
CLIPS = 24
GROUPS = 6
ROPE_BASE = 256.0
NORM_EPS = 1e-06
MASKED = -30000.0
BF16 = jnp.bfloat16
F32 = jnp.float32


def rope_rows():
    table = np.zeros((8, HD), np.float32)
    lead = HD // 8
    side = (HD - lead) // 2
    offset = 0
    for section in (lead, side, side):
        middle = section // 2
        for column in range(section):
            within = column % middle
            table[0, offset + column] = ROPE_BASE ** (-2.0 * within / section)
            first = column < middle
            table[1, offset + column] = -1.0 if first else 1.0
            table[2, offset + column] = offset + column + (middle if first else -middle)
        offset += section
    return table


def group_base(group):
    return 1024 * group if group < 2 else 2048 + 512 * (group - 2)


def kernel(
    n_dp, q_parts, c_parts,
    x_ref, pos_ref, idx_ref, len_ref, grp_ref, qg_ref, kg_ref, w_ref, tab_ref,
    out_ref,
    send, recv, lab_send, lab_recv, osend, orecv, wfull, hot_q, hot_k, perm, acc,
    send_sem, recv_sem, lab_sems, ret_send, ret_recv, own_sem,
    wz_sems, xy_send, xy_recv, sib_sems,
):
    n = 32
    dp = lax.axis_index("dp")
    me = lax.axis_index("fsdp")
    core = me % 2
    chip = me // 2
    sibling = me + 1 - 2 * core
    q_part = dp // c_parts
    c_part = dp % c_parts
    w_rows, w_cols = 64 // q_parts, 1536 // c_parts

    def slot_of(row, side):
        return (row % c_parts) * (2 * q_parts) + side * q_parts + row // c_parts

    def far_first(step):
        near = n - 1 - step
        return (me + jnp.where(near % 2 == 1, (near + 1) // 2, n - near // 2)) % n

    barrier = pltpu.get_barrier_semaphore()

    @pl.loop(1, n)
    def _(i):
        pl.semaphore_signal(barrier, inc=1, device_id={"fsdp": (me + i) % n}, device_id_type=MESH)

    if n_dp > 1:
        @pl.loop(1, n_dp)
        def _(i):
            pl.semaphore_signal(barrier, inc=1, device_id={"dp": (dp + i) % n_dp}, device_id_type=MESH)

    idx = idx_ref[...].astype(F32)
    across = jnp.broadcast_to(idx, (HD, HD))
    down = across.T
    rank = jnp.sum((down < across).astype(F32), axis=0, keepdims=True)
    row_id = lax.broadcasted_iota(jnp.int32, (HD, HD), 0).astype(F32)
    lane_id = lax.broadcasted_iota(jnp.int32, (HD, HD), 1).astype(F32)
    rank_rows = jnp.broadcast_to(rank, (HD, HD))
    to_sorted = (rank_rows == row_id).astype(F32).astype(BF16)
    perm[...] = (rank_rows.T == lane_id).astype(F32).astype(BF16)

    running = [jnp.int32(group_base(g)) for g in range(GROUPS)]
    label = jnp.zeros((1, HD), F32)
    for clip in range(CLIPS):
        length, group = len_ref[clip], grp_ref[clip]
        end = jnp.int32(0)
        for g in range(GROUPS):
            inside = group == g
            running[g] = running[g] + jnp.where(inside, length, 0)
            end = end + jnp.where(inside, running[g], 0)
        label = label + (idx_ref[...] >= end).astype(F32)
    ordered = lax.dot_general(
        jnp.broadcast_to(label, (8, HD)).astype(BF16), to_sorted,
        (((1,), (1,)), ((), ())), preferred_element_type=F32,
    )
    lane = lax.broadcasted_iota(jnp.int32, (8, HD), 1)
    window = 32 * (me % 4)
    for g in range(GROUPS):
        if g < 2:
            shown = pltpu.roll(ordered, (window - 32 * g + HD) % HD, 1)
        else:
            first = 64 + 16 * (g - 2)
            low = pltpu.roll(ordered, (window - first + HD) % HD, 1)
            high = pltpu.roll(ordered, (window + 16 - first + HD) % HD, 1) + 32.0
            shown = jnp.where(lane >= window + 16, high, low)
        shown = jnp.where((lane >= window) & (lane < window + 32), shown, 0.0)
        lab_send[g] = shown[0:1]

    freq = tab_ref[0:1, :]
    sign = tab_ref[1:2, :]
    swap = (jnp.broadcast_to(tab_ref[2:3, :], (HD, HD)) == row_id).astype(F32)
    pos = pos_ref[...].astype(F32)
    section = jnp.where(
        row_id < 16, pos[0:1, :], jnp.where(row_id < 72, pos[1:2, :], pos[2:3, :])
    ).astype(BF16)
    place = lax.dot_general(
        to_sorted, section, (((1,), (1,)), ((), ())), preferred_element_type=F32
    )
    angles = place * freq
    cosine = jnp.cos(angles)
    sine = jnp.sin(angles) * sign
    swap_b = swap.astype(BF16)
    tables = []
    for gain_ref in (qg_ref, kg_ref):
        gain = gain_ref[...]
        gain_down = jnp.broadcast_to(gain, (HD, HD)).T
        turned = jnp.sum(gain_down * swap, axis=0, keepdims=True)
        tables.append((cosine * gain, sine * turned))

    pl.semaphore_wait(barrier, n - 1 + (n_dp - 1))

    def w_mine():
        return w_ref.at[
            pl.ds(pl.multiple_of(q_part * w_rows, w_rows), w_rows),
            pl.ds(pl.multiple_of(c_part * w_cols, w_cols), w_cols),
        ]

    my_slot = slot_of(dp, core)
    w_place = wfull.at[chip // 2, chip % 2, my_slot]
    w_own = pltpu.make_async_copy(w_mine(), w_place, own_sem.at[0])
    w_own.start()

    @pl.loop(1, 16)
    def _(i):
        pltpu.make_async_remote_copy(
            src_ref=w_mine(), dst_ref=w_place, send_sem=wz_sems.at[0], recv_sem=wz_sems.at[1],
            device_id={"fsdp": 2 * ((chip + i) % 16) + core}, device_id_type=MESH,
        ).start()

    def group_of(peer):
        return jnp.where(peer < 16, peer // 8, 2 + (peer - 16) // 4)

    @pl.loop(0, n - 1)
    def _(i):
        peer = far_first(i)
        pltpu.make_async_remote_copy(
            src_ref=lab_send.at[group_of(peer)], dst_ref=lab_recv.at[me],
            send_sem=lab_sems.at[0], recv_sem=lab_sems.at[1],
            device_id={"fsdp": peer}, device_id_type=MESH,
        ).start()

    lab_own = pltpu.make_async_copy(lab_send.at[group_of(me)], lab_recv.at[me], own_sem.at[1])
    lab_own.start()

    def prepare(half):
        def one(m, carry):
            columns = pl.ds(pl.multiple_of((2 * m + half) * HD, HD), HD)
            for kind in range(3):
                entries = jnp.dot(to_sorted, x_ref[kind, :, columns], preferred_element_type=F32)
                if kind < 2:
                    cos_gain, sin_gain = tables[kind]
                    swapped = jnp.dot(entries.astype(BF16), swap_b, preferred_element_type=F32)
                    mean = jnp.sum(entries * entries, axis=1, keepdims=True) * (1.0 / HD)
                    factor = lax.rsqrt(mean + NORM_EPS)
                    entries = (entries * cos_gain + swapped * sin_gain) * factor
                rows = entries.astype(BF16)
                for g in range(2):
                    send[half, 8 * g + m, kind] = rows[32 * g:32 * g + 32]
                for g in range(4):
                    send[half, 16 + 4 * g + m // 2, kind, pl.ds(pl.multiple_of(16 * (m % 2), 16), 16)] = (
                        rows[64 + 16 * g:80 + 16 * g]
                    )
            return carry

        lax.fori_loop(0, 8, one, 0)

        @pl.loop(0, n - 1)
        def _(i):
            peer = far_first(i)
            pltpu.make_async_remote_copy(
                src_ref=send.at[half, peer], dst_ref=recv.at[half, me],
                send_sem=send_sem.at[half], recv_sem=recv_sem.at[half],
                device_id={"fsdp": peer}, device_id_type=MESH,
            ).start()

        copy = pltpu.make_async_copy(send.at[half, me], recv.at[half, me], own_sem.at[2 + half])
        copy.start()
        return copy

    own_first = prepare(0)

    def ring_total():
        return wfull.at[:, :, 0]

    def ring_wait():
        view = wfull.at[pl.ds(0, 5), pl.ds(0, 1), pl.ds(0, 3)]
        return pltpu.make_async_remote_copy(
            src_ref=view, dst_ref=view, send_sem=wz_sems.at[0], recv_sem=wz_sems.at[1],
            device_id={"fsdp": sibling}, device_id_type=MESH,
        )

    w_own.wait()
    if q_parts * c_parts > 1:
        ring_wait().wait_recv()
    else:
        @pl.loop(1, 16)
        def _(i):
            pltpu.make_async_remote_copy(
                src_ref=w_mine(), dst_ref=w_place, send_sem=wz_sems.at[0], recv_sem=wz_sems.at[1],
                device_id={"fsdp": sibling}, device_id_type=MESH,
            ).wait_recv()

    def xy_copy(to, source):
        part = wfull.at[:, :, slot_of(source, core)]
        return pltpu.make_async_remote_copy(
            src_ref=part, dst_ref=part, send_sem=xy_send, recv_sem=xy_recv.at[source],
            device_id={"dp": to}, device_id_type=MESH,
        )

    if n_dp > 1:
        @pl.loop(1, n_dp)
        def _(i):
            xy_copy((dp + i) % n_dp, dp).start()

    def sib_copy(source):
        part = wfull.at[:, :, slot_of(source, core)]
        return pltpu.make_async_remote_copy(
            src_ref=part, dst_ref=part, send_sem=sib_sems.at[0], recv_sem=sib_sems.at[1],
            device_id={"fsdp": sibling}, device_id_type=MESH,
        )

    sib_copy(dp).start()

    own_second = prepare(1)

    def label_wait():
        view = lab_recv.at[pl.ds(0, n - 1)]
        return pltpu.make_async_remote_copy(
            src_ref=view, dst_ref=view, send_sem=lab_sems.at[0], recv_sem=lab_sems.at[1],
            device_id={"fsdp": sibling}, device_id_type=MESH,
        )

    lab_own.wait()
    label_wait().wait_recv()
    for block in range(8):
        row = lab_recv[4 * block] + lab_recv[4 * block + 1] + lab_recv[4 * block + 2] + lab_recv[4 * block + 3]
        same = jnp.broadcast_to(row, (HD, HD)).T == lane_id
        hot_q[block * HD:(block + 1) * HD] = jnp.where(same, 1.0, 0.0).astype(BF16)
        hot_k[block * HD:(block + 1) * HD] = jnp.where(same, 0.0, MASKED).astype(BF16)

    def half_wait(half):
        view = recv.at[half, pl.ds(0, n - 1)]
        return pltpu.make_async_remote_copy(
            src_ref=view, dst_ref=view, send_sem=send_sem.at[half], recv_sem=recv_sem.at[half],
            device_id={"fsdp": sibling}, device_id_type=MESH,
        )

    def back_wait(half):
        view = orecv.at[half, pl.ds(0, n - 1)]
        return pltpu.make_async_remote_copy(
            src_ref=view, dst_ref=view, send_sem=ret_send.at[half], recv_sem=ret_recv.at[half],
            device_id={"fsdp": sibling}, device_id_type=MESH,
        )

    scale = math.log2(math.e) / math.sqrt(HD)

    def attend(half, own_copy):
        own_copy.wait()
        half_wait(half).wait_recv()

        def block(step, carry):
            turn = jnp.where(step == 0, 2, jnp.where(step == 1, 1, jnp.where(step == 2, 3, 0)))
            part = (me // 8 + turn) % 4
            first = pl.multiple_of(8 * part, 8)
            queries = jnp.concatenate(
                [recv[half, pl.ds(first, 8), 0].reshape(256, HD),
                 hot_q[pl.ds(pl.multiple_of(256 * part, 256), 256)]], axis=1)
            total = jnp.zeros((256, 2 * HD), F32)
            for key_part in range(4):
                keys = jnp.concatenate(
                    [recv[half, 8 * key_part:8 * key_part + 8, 1].reshape(256, HD),
                     hot_k[256 * key_part:256 * key_part + 256]], axis=1)
                values = jnp.concatenate(
                    [recv[half, 8 * key_part:8 * key_part + 8, 2].reshape(256, HD),
                     jnp.ones((256, HD), BF16)], axis=1)
                scores = lax.dot_general(
                    queries, keys, (((1,), (1,)), ((), ())), preferred_element_type=F32)
                weights = jnp.exp2(scores * scale).astype(BF16)
                total = total + jnp.dot(weights, values, preferred_element_type=F32)
            result = (total[:, :HD] / total[:, HD:]).astype(BF16)
            osend[half, pl.ds(first, 8)] = result.reshape(8, 32, HD)

            @pl.loop(0, 8)
            def _(i):
                peer = first + (me + i) % 8

                @pl.when(peer != me)
                def _():
                    pltpu.make_async_remote_copy(
                        src_ref=osend.at[half, peer], dst_ref=orecv.at[half, me],
                        send_sem=ret_send.at[half], recv_sem=ret_recv.at[half],
                        device_id={"fsdp": peer}, device_id_type=MESH,
                    ).start()
            return carry

        lax.fori_loop(0, 4, block, 0)
        copy = pltpu.make_async_copy(osend.at[half, me], orecv.at[half, me], own_sem.at[4 + half])
        copy.start()
        return copy

    back_first = attend(0, own_first)

    if n_dp > 1:
        @pl.loop(1, n_dp)
        def _(i):
            source = (dp + n_dp - i) % n_dp
            xy_copy(dp, source).wait_recv()
            sib_copy(source).start()

    back_second = attend(1, own_second)

    def sib_wait():
        view = wfull.at[:, :, pl.ds(0, n_dp)]
        return pltpu.make_async_remote_copy(
            src_ref=view, dst_ref=view, send_sem=sib_sems.at[0], recv_sem=sib_sems.at[1],
            device_id={"fsdp": sibling}, device_id_type=MESH,
        )

    sib_wait().wait_recv()

    def gathered(half):
        heads = []
        for m in range(8):
            parts = [orecv[half, m], orecv[half, 8 + m]]
            for g in range(4):
                parts.append(orecv[half, 16 + 4 * g + m // 2, 16 * (m % 2):16 * (m % 2) + 16])
            heads.append(jnp.concatenate(parts, axis=0))
        return jnp.concatenate(heads, axis=1)

    def project(half, c):
        rows = wfull[:, half, 2 * q_parts * c:2 * q_parts * (c + 1)].reshape(8 * HD, w_cols)
        return rows

    back_first.wait()
    back_wait(0).wait_recv()
    left = gathered(0)
    for c in range(c_parts):
        acc[:, c * w_cols:(c + 1) * w_cols] = jnp.dot(left, project(0, c), preferred_element_type=F32)
    back_second.wait()
    back_wait(1).wait_recv()
    left = gathered(1)
    for c in range(c_parts):
        columns = slice(c * w_cols, (c + 1) * w_cols)
        mixed = acc[:, columns] + jnp.dot(left, project(1, c), preferred_element_type=F32)
        out_ref[:, columns] = jnp.dot(
            perm[...], mixed.astype(BF16), preferred_element_type=F32
        ).astype(BF16)

    for half in range(2):
        half_wait(half).wait_send()
        back_wait(half).wait_send()
    label_wait().wait_send()
    if q_parts * c_parts > 1:
        ring_wait().wait_send()
    else:
        @pl.loop(1, 16)
        def _(i):
            pltpu.make_async_remote_copy(
                src_ref=w_mine(), dst_ref=w_place, send_sem=wz_sems.at[0], recv_sem=wz_sems.at[1],
                device_id={"fsdp": sibling}, device_id_type=MESH,
            ).wait_send()
    if n_dp > 1:
        view = wfull.at[:, :, pl.ds(0, n_dp - 1)]
        pltpu.make_async_remote_copy(
            src_ref=view, dst_ref=view, send_sem=xy_send, recv_sem=xy_recv.at[0],
            device_id={"fsdp": sibling}, device_id_type=MESH,
        ).wait_send()
    sib_wait().wait_send()


def on_device(n_dp, projections, positions, packed_index, clip_length, clip_group, query_gain, key_gain, out_weight):
    q_parts, c_parts = {16: (4, 4), 2: (1, 2), 1: (1, 1)}[n_dp]
    vmem = pl.BlockSpec(memory_space=pltpu.VMEM)
    smem = pl.BlockSpec(memory_space=pltpu.SMEM)
    dma = pltpu.SemaphoreType.DMA
    return pl.pallas_call(
        functools.partial(kernel, n_dp, q_parts, c_parts),
        out_shape=jax.ShapeDtypeStruct((128, 1536), BF16),
        in_specs=[vmem, vmem, vmem, smem, smem, vmem, vmem, vmem, vmem],
        out_specs=vmem,
        scratch_shapes=[
            pltpu.VMEM((2, 32, 3, 32, HD), BF16),
            pltpu.VMEM((2, 32, 3, 32, HD), BF16),
            pltpu.VMEM((GROUPS, 1, HD), F32),
            pltpu.VMEM((32, 1, HD), F32),
            pltpu.VMEM((2, 32, 32, HD), BF16),
            pltpu.VMEM((2, 32, 32, HD), BF16),
            pltpu.VMEM((8, 2, 2 * q_parts * c_parts, 64 // q_parts, 1536 // c_parts), BF16),
            pltpu.VMEM((8 * HD, HD), BF16),
            pltpu.VMEM((8 * HD, HD), BF16),
            pltpu.VMEM((HD, HD), BF16),
            pltpu.VMEM((HD, 1536), F32),
            dma((2,)),
            dma((2,)),
            dma((2,)),
            dma((2,)),
            dma((2,)),
            dma((6,)),
            dma((2,)),
            dma,
            dma((n_dp,)),
            dma((2,)),
        ],
        compiler_params=pltpu.CompilerParams(
            collective_id=0, has_side_effects=True, vmem_limit_bytes=40 * 1024 * 1024
        ),
        cost_estimate=pl.CostEstimate(flops=3_500_000_000, bytes_accessed=4_000_000, transcendentals=2_500_000),
    )(
        projections.transpose(1, 0, 2),
        positions,
        packed_index.reshape(1, 128),
        clip_length,
        clip_group,
        query_gain.reshape(1, HD),
        key_gain.reshape(1, HD),
        out_weight,
        jnp.asarray(rope_rows()),
    )


def solution(mesh):
    placed = (
        P(("dp", "fsdp"), None, None),
        P(None, ("dp", "fsdp")),
        P(("dp", "fsdp")),
        P("dp"),
        P("dp"),
        P(),
        P(),
        P("fsdp", None),
    )
    return jax.shard_map(
        functools.partial(on_device, mesh.shape["dp"]),
        mesh=mesh, in_specs=placed, out_specs=P(("dp", "fsdp"), None), check_vma=False,
    )
```

```python
import functools
import math

import jax
import jax.numpy as jnp
import numpy as np
from jax import lax
from jax.experimental import pallas as pl
from jax.experimental.pallas import tpu as pltpu
from jax.sharding import PartitionSpec as P

MESH = pl.DeviceIdType.MESH
HD = 128
CLIPS = 24
GROUPS = 6
ROPE_BASE = 256.0
NORM_EPS = 1e-06
MASKED = -30000.0
BF16 = jnp.bfloat16
F32 = jnp.float32


def rope_rows():
    table = np.zeros((8, HD), np.float32)
    lead = HD // 8
    side = (HD - lead) // 2
    offset = 0
    for section in (lead, side, side):
        middle = section // 2
        for column in range(section):
            within = column % middle
            table[0, offset + column] = ROPE_BASE ** (-2.0 * within / section)
            first = column < middle
            table[1, offset + column] = -1.0 if first else 1.0
            table[2, offset + column] = offset + column + (middle if first else -middle)
        offset += section
    return table


def group_base(group):
    return 1024 * group if group < 2 else 2048 + 512 * (group - 2)


def kernel(
    n_dp, q_parts, c_parts,
    x_hbm, pos_hbm, idx_hbm, len_hbm, grp_hbm, qg_hbm, kg_hbm, w_ref, tab_hbm,
    out_ref,
    x_ref, pos_ref, idx_ref, len_ref, grp_ref, qg_ref, kg_ref, tab_ref, in_sems,
    send, recv, lab_send, lab_recv, osend, orecv, wfull, hot_q, hot_k, perm, acc,
    send_sem, recv_sem, lab_sems, ret_send, ret_recv, own_sem,
    wz_sems, xy_send, xy_recv, sib_sems,
):
    n = 32
    dp = lax.axis_index("dp")
    me = lax.axis_index("fsdp")
    core = me % 2
    chip = me // 2
    sibling = me + 1 - 2 * core
    q_part = dp // c_parts
    c_part = dp % c_parts
    w_rows, w_cols = 64 // q_parts, 1536 // c_parts

    def slot_of(row, side):
        return (row % c_parts) * (2 * q_parts) + side * q_parts + row // c_parts

    def far_first(step):
        near = n - 1 - step
        return (me + jnp.where(near % 2 == 1, (near + 1) // 2, n - near // 2)) % n

    barrier = pltpu.get_barrier_semaphore()

    @pl.loop(1, n)
    def _(i):
        pl.semaphore_signal(barrier, inc=1, device_id={"fsdp": (me + i) % n}, device_id_type=MESH)

    if n_dp > 1:
        @pl.loop(1, n_dp)
        def _(i):
            pl.semaphore_signal(barrier, inc=1, device_id={"dp": (dp + i) % n_dp}, device_id_type=MESH)

    arrivals = [
        pltpu.make_async_copy(source, target, in_sems.at[i])
        for i, (source, target) in enumerate((
            (idx_hbm, idx_ref), (len_hbm, len_ref), (grp_hbm, grp_ref), (pos_hbm, pos_ref),
            (qg_hbm, qg_ref), (kg_hbm, kg_ref), (tab_hbm, tab_ref), (x_hbm, x_ref),
        ))
    ]
    for arrival in arrivals:
        arrival.start()
    for arrival in arrivals[:-1]:
        arrival.wait()

    idx = idx_ref[...].astype(F32)
    across = jnp.broadcast_to(idx, (HD, HD))
    down = across.T
    rank = jnp.sum((down < across).astype(F32), axis=0, keepdims=True)
    row_id = lax.broadcasted_iota(jnp.int32, (HD, HD), 0).astype(F32)
    lane_id = lax.broadcasted_iota(jnp.int32, (HD, HD), 1).astype(F32)
    rank_rows = jnp.broadcast_to(rank, (HD, HD))
    to_sorted = (rank_rows == row_id).astype(F32).astype(BF16)
    perm[...] = (rank_rows.T == lane_id).astype(F32).astype(BF16)

    running = [jnp.int32(group_base(g)) for g in range(GROUPS)]
    label = jnp.zeros((1, HD), F32)
    for clip in range(CLIPS):
        length, group = len_ref[clip], grp_ref[clip]
        end = jnp.int32(0)
        for g in range(GROUPS):
            inside = group == g
            running[g] = running[g] + jnp.where(inside, length, 0)
            end = end + jnp.where(inside, running[g], 0)
        label = label + (idx_ref[...] >= end).astype(F32)
    ordered = lax.dot_general(
        jnp.broadcast_to(label, (8, HD)).astype(BF16), to_sorted,
        (((1,), (1,)), ((), ())), preferred_element_type=F32,
    )
    lane = lax.broadcasted_iota(jnp.int32, (8, HD), 1)
    window = 32 * (me % 4)
    for g in range(GROUPS):
        if g < 2:
            shown = pltpu.roll(ordered, (window - 32 * g + HD) % HD, 1)
        else:
            first = 64 + 16 * (g - 2)
            low = pltpu.roll(ordered, (window - first + HD) % HD, 1)
            high = pltpu.roll(ordered, (window + 16 - first + HD) % HD, 1) + 32.0
            shown = jnp.where(lane >= window + 16, high, low)
        shown = jnp.where((lane >= window) & (lane < window + 32), shown, 0.0)
        lab_send[g] = shown[0:1]

    freq = tab_ref[0:1, :]
    sign = tab_ref[1:2, :]
    swap = (jnp.broadcast_to(tab_ref[2:3, :], (HD, HD)) == row_id).astype(F32)
    pos = pos_ref[...].astype(F32)
    section = jnp.where(
        row_id < 16, pos[0:1, :], jnp.where(row_id < 72, pos[1:2, :], pos[2:3, :])
    ).astype(BF16)
    place = lax.dot_general(
        to_sorted, section, (((1,), (1,)), ((), ())), preferred_element_type=F32
    )
    angles = place * freq
    cosine = jnp.cos(angles)
    sine = jnp.sin(angles) * sign
    swap_b = swap.astype(BF16)
    tables = []
    for gain_ref in (qg_ref, kg_ref):
        gain = gain_ref[...]
        gain_down = jnp.broadcast_to(gain, (HD, HD)).T
        turned = jnp.sum(gain_down * swap, axis=0, keepdims=True)
        tables.append((cosine * gain, sine * turned))

    def prepare(half):
        def one(m, carry):
            columns = pl.ds(pl.multiple_of((2 * m + half) * HD, HD), HD)
            for kind in range(3):
                entries = jnp.dot(to_sorted, x_ref[kind, :, columns], preferred_element_type=F32)
                if kind < 2:
                    cos_gain, sin_gain = tables[kind]
                    swapped = jnp.dot(entries.astype(BF16), swap_b, preferred_element_type=F32)
                    mean = jnp.sum(entries * entries, axis=1, keepdims=True) * (1.0 / HD)
                    factor = lax.rsqrt(mean + NORM_EPS)
                    entries = (entries * cos_gain + swapped * sin_gain) * factor
                rows = entries.astype(BF16)
                for g in range(2):
                    send[half, 8 * g + m, kind] = rows[32 * g:32 * g + 32]
                for g in range(4):
                    send[half, 16 + 4 * g + m // 2, kind, pl.ds(pl.multiple_of(16 * (m % 2), 16), 16)] = (
                        rows[64 + 16 * g:80 + 16 * g]
                    )
            return carry

        lax.fori_loop(0, 8, one, 0)

    def send_some(half, first, last):
        @pl.loop(first, last)
        def _(i):
            peer = far_first(i)
            pltpu.make_async_remote_copy(
                src_ref=send.at[half, peer], dst_ref=recv.at[half, me],
                send_sem=send_sem.at[half], recv_sem=recv_sem.at[half],
                device_id={"fsdp": peer}, device_id_type=MESH,
            ).start()

    def keep_own(half):
        copy = pltpu.make_async_copy(send.at[half, me], recv.at[half, me], own_sem.at[2 + half])
        copy.start()
        return copy

    arrivals[-1].wait()
    prepare(0)
    my_slot = slot_of(dp, core)
    w_own = pltpu.make_async_copy(
        w_ref.at[
            pl.ds(pl.multiple_of(q_part * w_rows, w_rows), w_rows),
            pl.ds(pl.multiple_of(c_part * w_cols, w_cols), w_cols),
        ],
        wfull.at[chip // 4, (chip // 2) % 2, chip % 2, my_slot], own_sem.at[0],
    )
    w_own.start()
    pl.semaphore_wait(barrier, n - 1 + (n_dp - 1))

    def far_w(k):
        away = (8, 4, 12)[k]
        piece = wfull.at[chip // 4, (chip // 2) % 2, chip % 2, my_slot]
        return pltpu.make_async_remote_copy(
            src_ref=piece, dst_ref=piece, send_sem=wz_sems.at[0, k], recv_sem=wz_sems.at[1, k],
            device_id={"fsdp": 2 * ((chip + away) % 16) + core}, device_id_type=MESH,
        )

    def near_w(k):
        away = (2, 1, 15)[k]
        pieces = wfull.at[:, (chip // 2) % 2, chip % 2, my_slot]
        return pltpu.make_async_remote_copy(
            src_ref=pieces, dst_ref=pieces, send_sem=wz_sems.at[2, k], recv_sem=wz_sems.at[3, k],
            device_id={"fsdp": 2 * ((chip + away) % 16) + core}, device_id_type=MESH,
        )

    w_own.wait()
    for k in range(3):
        far_w(k).start()
    send_some(0, 0, 16)
    own_first = keep_own(0)
    prepare(1)
    for k in range(3):
        far_w(k).wait_recv()
    for k in range(3):
        near_w(k).start()
    send_some(0, 16, n - 1)

    def group_of(peer):
        return jnp.where(peer < 16, peer // 8, 2 + (peer - 16) // 4)

    @pl.loop(0, n - 1)
    def _(i):
        peer = far_first(i)
        pltpu.make_async_remote_copy(
            src_ref=lab_send.at[group_of(peer)], dst_ref=lab_recv.at[me],
            send_sem=lab_sems.at[0], recv_sem=lab_sems.at[1],
            device_id={"fsdp": peer}, device_id_type=MESH,
        ).start()

    lab_own = pltpu.make_async_copy(lab_send.at[group_of(me)], lab_recv.at[me], own_sem.at[1])
    lab_own.start()

    own_second = keep_own(1)
    for k in range(3):
        near_w(k).wait_recv()

    def xy_copy(to, source):
        part = wfull.at[:, :, :, slot_of(source, core)]
        return pltpu.make_async_remote_copy(
            src_ref=part, dst_ref=part, send_sem=xy_send, recv_sem=xy_recv.at[source],
            device_id={"dp": to}, device_id_type=MESH,
        )

    if n_dp > 1:
        @pl.loop(1, n_dp)
        def _(i):
            xy_copy((dp + i) % n_dp, dp).start()

    def sib_copy(source):
        part = wfull.at[:, :, :, slot_of(source, core)]
        return pltpu.make_async_remote_copy(
            src_ref=part, dst_ref=part, send_sem=sib_sems.at[0], recv_sem=sib_sems.at[1],
            device_id={"fsdp": sibling}, device_id_type=MESH,
        )

    sib_copy(dp).start()
    send_some(1, 0, n - 1)

    def label_wait():
        view = lab_recv.at[pl.ds(0, n - 1)]
        return pltpu.make_async_remote_copy(
            src_ref=view, dst_ref=view, send_sem=lab_sems.at[0], recv_sem=lab_sems.at[1],
            device_id={"fsdp": sibling}, device_id_type=MESH,
        )

    lab_own.wait()
    label_wait().wait_recv()
    for block in range(8):
        row = lab_recv[4 * block] + lab_recv[4 * block + 1] + lab_recv[4 * block + 2] + lab_recv[4 * block + 3]
        same = jnp.broadcast_to(row, (HD, HD)).T == lane_id
        hot_q[block * HD:(block + 1) * HD] = jnp.where(same, 1.0, 0.0).astype(BF16)
        hot_k[block * HD:(block + 1) * HD] = jnp.where(same, 0.0, MASKED).astype(BF16)

    def half_wait(half):
        view = recv.at[half, pl.ds(0, n - 1)]
        return pltpu.make_async_remote_copy(
            src_ref=view, dst_ref=view, send_sem=send_sem.at[half], recv_sem=recv_sem.at[half],
            device_id={"fsdp": sibling}, device_id_type=MESH,
        )

    def back_wait(half):
        view = orecv.at[half, pl.ds(0, n - 1)]
        return pltpu.make_async_remote_copy(
            src_ref=view, dst_ref=view, send_sem=ret_send.at[half], recv_sem=ret_recv.at[half],
            device_id={"fsdp": sibling}, device_id_type=MESH,
        )

    scale = math.log2(math.e) / math.sqrt(HD)

    def attend(half, own_copy):
        own_copy.wait()
        half_wait(half).wait_recv()

        def block(part, carry):
            first = pl.multiple_of(8 * part, 8)
            queries = jnp.concatenate(
                [recv[half, pl.ds(first, 8), 0].reshape(256, HD),
                 hot_q[pl.ds(pl.multiple_of(256 * part, 256), 256)]], axis=1)
            total = jnp.zeros((256, 2 * HD), F32)
            for key_part in range(4):
                keys = jnp.concatenate(
                    [recv[half, 8 * key_part:8 * key_part + 8, 1].reshape(256, HD),
                     hot_k[256 * key_part:256 * key_part + 256]], axis=1)
                values = jnp.concatenate(
                    [recv[half, 8 * key_part:8 * key_part + 8, 2].reshape(256, HD),
                     jnp.ones((256, HD), BF16)], axis=1)
                scores = lax.dot_general(
                    queries, keys, (((1,), (1,)), ((), ())), preferred_element_type=F32)
                weights = jnp.exp2(scores * scale).astype(BF16)
                total = total + jnp.dot(weights, values, preferred_element_type=F32)
            result = (total[:, :HD] / total[:, HD:]).astype(BF16)
            osend[half, pl.ds(first, 8)] = result.reshape(8, 32, HD)

            return carry

        lax.fori_loop(0, 4, block, 0)

        @pl.loop(0, n - 1)
        def _(i):
            peer = far_first(i)
            pltpu.make_async_remote_copy(
                src_ref=osend.at[half, peer], dst_ref=orecv.at[half, me],
                send_sem=ret_send.at[half], recv_sem=ret_recv.at[half],
                device_id={"fsdp": peer}, device_id_type=MESH,
            ).start()

        copy = pltpu.make_async_copy(osend.at[half, me], orecv.at[half, me], own_sem.at[4 + half])
        copy.start()
        return copy

    back_first = attend(0, own_first)

    if n_dp > 1:
        @pl.loop(1, n_dp)
        def _(i):
            source = (dp + n_dp - i) % n_dp
            xy_copy(dp, source).wait_recv()
            sib_copy(source).start()

    back_second = attend(1, own_second)

    def sib_wait():
        view = wfull.at[:, :, :, pl.ds(0, n_dp)]
        return pltpu.make_async_remote_copy(
            src_ref=view, dst_ref=view, send_sem=sib_sems.at[0], recv_sem=sib_sems.at[1],
            device_id={"fsdp": sibling}, device_id_type=MESH,
        )

    sib_wait().wait_recv()

    def gathered(half):
        heads = []
        for m in range(8):
            parts = [orecv[half, m], orecv[half, 8 + m]]
            for g in range(4):
                parts.append(orecv[half, 16 + 4 * g + m // 2, 16 * (m % 2):16 * (m % 2) + 16])
            heads.append(jnp.concatenate(parts, axis=0))
        return jnp.concatenate(heads, axis=1)

    def project(half, c):
        rows = wfull[:, :, half, 2 * q_parts * c:2 * q_parts * (c + 1)].reshape(8 * HD, w_cols)
        return rows

    back_first.wait()
    back_wait(0).wait_recv()
    left = gathered(0)
    for c in range(c_parts):
        acc[:, c * w_cols:(c + 1) * w_cols] = jnp.dot(left, project(0, c), preferred_element_type=F32)
    back_second.wait()
    back_wait(1).wait_recv()
    left = gathered(1)
    for c in range(c_parts):
        columns = slice(c * w_cols, (c + 1) * w_cols)
        mixed = acc[:, columns] + jnp.dot(left, project(1, c), preferred_element_type=F32)
        out_ref[:, columns] = jnp.dot(
            perm[...], mixed.astype(BF16), preferred_element_type=F32
        ).astype(BF16)

    for half in range(2):
        half_wait(half).wait_send()
        back_wait(half).wait_send()
    label_wait().wait_send()
    for k in range(3):
        far_w(k).wait_send()
    for k in range(3):
        near_w(k).wait_send()

    if n_dp > 1:
        view = wfull.at[:, :, :, pl.ds(0, n_dp - 1)]
        pltpu.make_async_remote_copy(
            src_ref=view, dst_ref=view, send_sem=xy_send, recv_sem=xy_recv.at[0],
            device_id={"fsdp": sibling}, device_id_type=MESH,
        ).wait_send()
    sib_wait().wait_send()


def on_device(n_dp, projections, positions, packed_index, clip_length, clip_group, query_gain, key_gain, out_weight):
    q_parts, c_parts = {16: (4, 4), 2: (1, 2), 1: (1, 1)}[n_dp]
    hbm = pl.BlockSpec(memory_space=pltpu.HBM)
    vmem = pl.BlockSpec(memory_space=pltpu.VMEM)
    dma = pltpu.SemaphoreType.DMA
    return pl.pallas_call(
        functools.partial(kernel, n_dp, q_parts, c_parts),
        out_shape=jax.ShapeDtypeStruct((128, 1536), BF16),
        in_specs=[hbm] * 9,
        out_specs=vmem,
        scratch_shapes=[
            pltpu.VMEM((3, 128, 2048), BF16),
            pltpu.VMEM((3, 128), jnp.int32),
            pltpu.VMEM((1, 128), jnp.int32),
            pltpu.SMEM((CLIPS,), jnp.int32),
            pltpu.SMEM((CLIPS,), jnp.int32),
            pltpu.VMEM((1, HD), F32),
            pltpu.VMEM((1, HD), F32),
            pltpu.VMEM((8, HD), F32),
            dma((8,)),
            pltpu.VMEM((2, 32, 3, 32, HD), BF16),
            pltpu.VMEM((2, 32, 3, 32, HD), BF16),
            pltpu.VMEM((GROUPS, 1, HD), F32),
            pltpu.VMEM((32, 1, HD), F32),
            pltpu.VMEM((2, 32, 32, HD), BF16),
            pltpu.VMEM((2, 32, 32, HD), BF16),
            pltpu.VMEM((4, 2, 2, 2 * q_parts * c_parts, 64 // q_parts, 1536 // c_parts), BF16),
            pltpu.VMEM((8 * HD, HD), BF16),
            pltpu.VMEM((8 * HD, HD), BF16),
            pltpu.VMEM((HD, HD), BF16),
            pltpu.VMEM((HD, 1536), F32),
            dma((2,)),
            dma((2,)),
            dma((2,)),
            dma((2,)),
            dma((2,)),
            dma((6,)),
            dma((4, 3)),
            dma,
            dma((n_dp,)),
            dma((2,)),
        ],
        compiler_params=pltpu.CompilerParams(
            collective_id=0, has_side_effects=True, vmem_limit_bytes=60 * 1024 * 1024
        ),
        cost_estimate=pl.CostEstimate(flops=3_500_000_000, bytes_accessed=4_000_000, transcendentals=2_500_000),
    )(
        projections.transpose(1, 0, 2),
        positions,
        packed_index.reshape(1, 128),
        clip_length,
        clip_group,
        query_gain.reshape(1, HD),
        key_gain.reshape(1, HD),
        out_weight,
        jnp.asarray(rope_rows()),
    )


def solution(mesh):
    placed = (
        P(("dp", "fsdp"), None, None),
        P(None, ("dp", "fsdp")),
        P(("dp", "fsdp")),
        P("dp"),
        P("dp"),
        P(),
        P(),
        P("fsdp", None),
    )
    return jax.shard_map(
        functools.partial(on_device, mesh.shape["dp"]),
        mesh=mesh, in_specs=placed, out_specs=P(("dp", "fsdp"), None), check_vma=False,
    )
```

```python
import functools
import math

import jax
import jax.numpy as jnp
import numpy as np
from jax import lax
from jax.experimental import pallas as pl
from jax.experimental.pallas import tpu as pltpu
from jax.sharding import PartitionSpec as P

MESH = pl.DeviceIdType.MESH
HD = 128
CLIPS = 24
GROUPS = 6
ROPE_BASE = 256.0
NORM_EPS = 1e-06
MASKED = -30000.0
BF16 = jnp.bfloat16
F32 = jnp.float32


def rope_rows():
    table = np.zeros((8, HD), np.float32)
    lead = HD // 8
    side = (HD - lead) // 2
    offset = 0
    for section in (lead, side, side):
        middle = section // 2
        for column in range(section):
            within = column % middle
            table[0, offset + column] = ROPE_BASE ** (-2.0 * within / section)
            first = column < middle
            table[1, offset + column] = -1.0 if first else 1.0
            table[2, offset + column] = offset + column + (middle if first else -middle)
        offset += section
    return table


def group_base(group):
    return 1024 * group if group < 2 else 2048 + 512 * (group - 2)


def kernel(
    n_dp, q_parts, c_parts,
    x_hbm, pos_hbm, idx_hbm, len_hbm, grp_hbm, qg_hbm, kg_hbm, w_ref, tab_hbm,
    out_ref,
    x_ref, pos_ref, idx_ref, len_ref, grp_ref, qg_ref, kg_ref, tab_ref, in_sems,
    send, recv, lab_send, lab_recv, osend, orecv, wfull, hot_q, hot_k, perm, acc,
    send_sem, recv_sem, lab_sems, ret_send, ret_recv, own_sem,
    wz_sems, xy_send, xy_recv, sib_sems, ring_known, plane_known,
):
    n = 32
    dp = lax.axis_index("dp")
    me = lax.axis_index("fsdp")
    core = me % 2
    chip = me // 2
    sibling = me + 1 - 2 * core
    q_part = dp // c_parts
    c_part = dp % c_parts
    w_rows, w_cols = 64 // q_parts, 1536 // c_parts

    def slot_of(row, side):
        return (row % c_parts) * (2 * q_parts) + side * q_parts + row // c_parts

    def chip_at(away, side):
        return 2 * ((chip + away + 16) % 16) + side

    def near_first(i):
        j = i + 3
        away = jnp.where((j // 2) % 2 == 0, j // 4, -(j // 4))
        return jnp.where(i == 0, sibling, chip_at(away, j % 2))

    def far_first(i):
        return near_first(n - 2 - i)

    def tell(semaphore, **place):
        pl.semaphore_signal(semaphore, inc=1, device_id=place, device_id_type=MESH)

    barrier = pltpu.get_barrier_semaphore()

    tell(barrier, fsdp=sibling)
    for away in (1, -1):
        for side in range(2):
            tell(barrier, fsdp=chip_at(away, side))
    if n_dp == 16:
        row, column = dp // 4, dp % 4
        for away in (1, 3):
            tell(barrier, dp=4 * row + (column + away) % 4)
            tell(barrier, dp=4 * ((row + away) % 4) + column)

    arrivals = [
        pltpu.make_async_copy(source, target, in_sems.at[i])
        for i, (source, target) in enumerate((
            (idx_hbm, idx_ref), (len_hbm, len_ref), (grp_hbm, grp_ref), (pos_hbm, pos_ref),
            (qg_hbm, qg_ref), (kg_hbm, kg_ref), (tab_hbm, tab_ref), (x_hbm, x_ref),
        ))
    ]
    for arrival in arrivals:
        arrival.start()
    for arrival in arrivals[:-1]:
        arrival.wait()

    idx = idx_ref[...].astype(F32)
    across = jnp.broadcast_to(idx, (HD, HD))
    down = across.T
    rank = jnp.sum((down < across).astype(F32), axis=0, keepdims=True)
    row_id = lax.broadcasted_iota(jnp.int32, (HD, HD), 0).astype(F32)
    lane_id = lax.broadcasted_iota(jnp.int32, (HD, HD), 1).astype(F32)
    rank_rows = jnp.broadcast_to(rank, (HD, HD))
    to_sorted = (rank_rows == row_id).astype(F32).astype(BF16)
    perm[...] = (rank_rows.T == lane_id).astype(F32).astype(BF16)

    running = [jnp.int32(group_base(g)) for g in range(GROUPS)]
    label = jnp.zeros((1, HD), F32)
    for clip in range(CLIPS):
        length, group = len_ref[clip], grp_ref[clip]
        end = jnp.int32(0)
        for g in range(GROUPS):
            inside = group == g
            running[g] = running[g] + jnp.where(inside, length, 0)
            end = end + jnp.where(inside, running[g], 0)
        label = label + (idx_ref[...] >= end).astype(F32)
    ordered = lax.dot_general(
        jnp.broadcast_to(label, (8, HD)).astype(BF16), to_sorted,
        (((1,), (1,)), ((), ())), preferred_element_type=F32,
    )
    lane = lax.broadcasted_iota(jnp.int32, (8, HD), 1)
    window = 32 * (me % 4)
    for g in range(GROUPS):
        if g < 2:
            shown = pltpu.roll(ordered, (window - 32 * g + HD) % HD, 1)
        else:
            first = 64 + 16 * (g - 2)
            low = pltpu.roll(ordered, (window - first + HD) % HD, 1)
            high = pltpu.roll(ordered, (window + 16 - first + HD) % HD, 1) + 32.0
            shown = jnp.where(lane >= window + 16, high, low)
        shown = jnp.where((lane >= window) & (lane < window + 32), shown, 0.0)
        lab_send[g] = shown[0:1]

    freq = tab_ref[0:1, :]
    sign = tab_ref[1:2, :]
    swap = (jnp.broadcast_to(tab_ref[2:3, :], (HD, HD)) == row_id).astype(F32)
    pos = pos_ref[...].astype(F32)
    section = jnp.where(
        row_id < 16, pos[0:1, :], jnp.where(row_id < 72, pos[1:2, :], pos[2:3, :])
    ).astype(BF16)
    place = lax.dot_general(
        to_sorted, section, (((1,), (1,)), ((), ())), preferred_element_type=F32
    )
    angles = place * freq
    cosine = jnp.cos(angles)
    sine = jnp.sin(angles) * sign
    swap_b = swap.astype(BF16)
    tables = []
    for gain_ref in (qg_ref, kg_ref):
        gain = gain_ref[...]
        gain_down = jnp.broadcast_to(gain, (HD, HD)).T
        turned = jnp.sum(gain_down * swap, axis=0, keepdims=True)
        tables.append((cosine * gain, sine * turned))

    def prepare(half):
        def one(m, carry):
            columns = pl.ds(pl.multiple_of((2 * m + half) * HD, HD), HD)
            for kind in range(3):
                entries = jnp.dot(to_sorted, x_ref[kind, :, columns], preferred_element_type=F32)
                if kind < 2:
                    cos_gain, sin_gain = tables[kind]
                    swapped = jnp.dot(entries.astype(BF16), swap_b, preferred_element_type=F32)
                    mean = jnp.sum(entries * entries, axis=1, keepdims=True) * (1.0 / HD)
                    factor = lax.rsqrt(mean + NORM_EPS)
                    entries = (entries * cos_gain + swapped * sin_gain) * factor
                rows = entries.astype(BF16)
                for g in range(2):
                    send[half, 8 * g + m, kind] = rows[32 * g:32 * g + 32]
                for g in range(4):
                    send[half, 16 + 4 * g + m // 2, kind, pl.ds(pl.multiple_of(16 * (m % 2), 16), 16)] = (
                        rows[64 + 16 * g:80 + 16 * g]
                    )
            return carry

        lax.fori_loop(0, 8, one, 0, unroll=8)

    def send_some(half, first, last, order=far_first):
        @pl.loop(first, last)
        def _(i):
            peer = order(i)
            pltpu.make_async_remote_copy(
                src_ref=send.at[half, peer], dst_ref=recv.at[half, me],
                send_sem=send_sem.at[half], recv_sem=recv_sem.at[half],
                device_id={"fsdp": peer}, device_id_type=MESH,
            ).start()

    def keep_own(half):
        copy = pltpu.make_async_copy(send.at[half, me], recv.at[half, me], own_sem.at[2 + half])
        copy.start()
        return copy

    arrivals[-1].wait()
    prepare(0)
    my_slot = slot_of(dp, core)
    w_own = pltpu.make_async_copy(
        w_ref.at[
            pl.ds(pl.multiple_of(q_part * w_rows, w_rows), w_rows),
            pl.ds(pl.multiple_of(c_part * w_cols, w_cols), w_cols),
        ],
        wfull.at[chip // 4, (chip // 2) % 2, chip % 2, my_slot], own_sem.at[0],
    )
    w_own.start()
    way = 1 - 2 * core

    def far_w(k):
        away = (4, 4, -4)[k] * way
        origin = chip if k else (chip - 4 * way + 16) % 16
        piece = wfull.at[origin // 4, (origin // 2) % 2, origin % 2, my_slot]
        return pltpu.make_async_remote_copy(
            src_ref=piece, dst_ref=piece, send_sem=wz_sems.at[0, k], recv_sem=wz_sems.at[1, k],
            device_id={"fsdp": chip_at(away, core)}, device_id_type=MESH,
        )

    def near_w(k):
        away = (2, 1, -1)[k] * way
        pieces = wfull.at[:, (chip // 2) % 2, chip % 2, my_slot]
        return pltpu.make_async_remote_copy(
            src_ref=pieces, dst_ref=pieces, send_sem=wz_sems.at[2, k], recv_sem=wz_sems.at[3, k],
            device_id={"fsdp": chip_at(away, core)}, device_id_type=MESH,
        )

    pl.semaphore_wait(barrier, 9 if n_dp == 16 else 5)
    for away in (1, -1):
        tell(ring_known.at[0], fsdp=chip_at(away, core))
    send_some(0, 0, 5, near_first)
    pl.semaphore_wait(ring_known.at[0], 2)
    for away in (2, -2):
        tell(ring_known.at[1], fsdp=chip_at(away, core))
    send_some(0, 5, 9, near_first)
    pl.semaphore_wait(ring_known.at[1], 2)
    for away in (4, -4):
        tell(ring_known.at[2], fsdp=chip_at(away, core))
    w_own.wait()
    far_w(1).start()
    far_w(2).start()
    send_some(0, 9, 17, near_first)
    own_first = keep_own(0)
    if n_dp == 16:
        for away in (1, 3):
            tell(plane_known.at[0], dp=4 * row + (column + away) % 4)
    prepare(1)
    own_second = keep_own(1)
    far_w(1).wait_recv()
    far_w(0).start()
    pl.semaphore_wait(ring_known.at[2], 2)
    send_some(0, 0, 2)
    if n_dp == 16:
        pl.semaphore_wait(plane_known.at[0], 2)
        for away in (1, 3):
            tell(plane_known.at[1], dp=4 * ((row + away) % 4) + column)
    far_w(2).wait_recv()
    far_w(0).wait_recv()
    for k in range(3):
        near_w(k).start()
    send_some(0, 2, 14)

    def group_of(peer):
        return jnp.where(peer < 16, peer // 8, 2 + (peer - 16) // 4)

    @pl.loop(0, n - 1)
    def _(i):
        peer = far_first(i)
        pltpu.make_async_remote_copy(
            src_ref=lab_send.at[group_of(peer)], dst_ref=lab_recv.at[me],
            send_sem=lab_sems.at[0], recv_sem=lab_sems.at[1],
            device_id={"fsdp": peer}, device_id_type=MESH,
        ).start()

    lab_own = pltpu.make_async_copy(lab_send.at[group_of(me)], lab_recv.at[me], own_sem.at[1])
    lab_own.start()

    send_some(1, 0, 12)
    for k in range(3):
        near_w(k).wait_recv()

    def xy_copy(to, source):
        part = wfull.at[:, :, :, slot_of(source, core)]
        return pltpu.make_async_remote_copy(
            src_ref=part, dst_ref=part, send_sem=xy_send, recv_sem=xy_recv.at[source],
            device_id={"dp": to}, device_id_type=MESH,
        )

    if n_dp == 16:
        pl.semaphore_wait(plane_known.at[1], 2)
        tell(plane_known.at[2], dp=4 * ((row + 2) % 4) + column)
        pl.semaphore_wait(plane_known.at[2], 1)

        @pl.loop(1, n_dp)
        def _(i):
            xy_copy((dp + i) % n_dp, dp).start()

    def sib_copy(source):
        part = wfull.at[:, :, :, slot_of(source, core)]
        return pltpu.make_async_remote_copy(
            src_ref=part, dst_ref=part, send_sem=sib_sems.at[0], recv_sem=sib_sems.at[1],
            device_id={"fsdp": sibling}, device_id_type=MESH,
        )

    sib_copy(dp).start()
    send_some(1, 12, n - 1)

    def label_wait():
        view = lab_recv.at[pl.ds(0, n - 1)]
        return pltpu.make_async_remote_copy(
            src_ref=view, dst_ref=view, send_sem=lab_sems.at[0], recv_sem=lab_sems.at[1],
            device_id={"fsdp": sibling}, device_id_type=MESH,
        )

    lab_own.wait()
    label_wait().wait_recv()
    for block in range(8):
        row = lab_recv[4 * block] + lab_recv[4 * block + 1] + lab_recv[4 * block + 2] + lab_recv[4 * block + 3]
        same = jnp.broadcast_to(row, (HD, HD)).T == lane_id
        hot_q[block * HD:(block + 1) * HD] = jnp.where(same, 1.0, 0.0).astype(BF16)
        hot_k[block * HD:(block + 1) * HD] = jnp.where(same, 0.0, MASKED).astype(BF16)

    def half_wait(half):
        view = recv.at[half, pl.ds(0, n - 1)]
        return pltpu.make_async_remote_copy(
            src_ref=view, dst_ref=view, send_sem=send_sem.at[half], recv_sem=recv_sem.at[half],
            device_id={"fsdp": sibling}, device_id_type=MESH,
        )

    def back_wait(half):
        view = orecv.at[half, pl.ds(0, n - 1)]
        return pltpu.make_async_remote_copy(
            src_ref=view, dst_ref=view, send_sem=ret_send.at[half], recv_sem=ret_recv.at[half],
            device_id={"fsdp": sibling}, device_id_type=MESH,
        )

    scale = math.log2(math.e) / math.sqrt(HD)

    def attend(half, own_copy):
        own_copy.wait()
        half_wait(half).wait_recv()

        def block(part, carry):
            first = pl.multiple_of(8 * part, 8)
            queries = jnp.concatenate(
                [recv[half, pl.ds(first, 8), 0].reshape(256, HD),
                 hot_q[pl.ds(pl.multiple_of(256 * part, 256), 256)]], axis=1)
            total = jnp.zeros((256, 2 * HD), F32)
            for key_part in range(4):
                keys = jnp.concatenate(
                    [recv[half, 8 * key_part:8 * key_part + 8, 1].reshape(256, HD),
                     hot_k[256 * key_part:256 * key_part + 256]], axis=1)
                values = jnp.concatenate(
                    [recv[half, 8 * key_part:8 * key_part + 8, 2].reshape(256, HD),
                     jnp.ones((256, HD), BF16)], axis=1)
                scores = lax.dot_general(
                    queries, keys, (((1,), (1,)), ((), ())), preferred_element_type=F32)
                weights = jnp.exp2(scores * scale).astype(BF16)
                total = total + jnp.dot(weights, values, preferred_element_type=F32)
            result = (total[:, :HD] / total[:, HD:]).astype(BF16)
            osend[half, pl.ds(first, 8)] = result.reshape(8, 32, HD)

            return carry

        lax.fori_loop(0, 4, block, 0)

        @pl.loop(0, n - 1)
        def _(i):
            peer = far_first(i)
            pltpu.make_async_remote_copy(
                src_ref=osend.at[half, peer], dst_ref=orecv.at[half, me],
                send_sem=ret_send.at[half], recv_sem=ret_recv.at[half],
                device_id={"fsdp": peer}, device_id_type=MESH,
            ).start()

        copy = pltpu.make_async_copy(osend.at[half, me], orecv.at[half, me], own_sem.at[4 + half])
        copy.start()
        return copy

    back_first = attend(0, own_first)

    if n_dp == 16:
        @pl.loop(1, n_dp)
        def _(i):
            source = (dp + n_dp - i) % n_dp
            xy_copy(dp, source).wait_recv()
            sib_copy(source).start()

    back_second = attend(1, own_second)

    def sib_wait():
        view = wfull.at[:, :, :, pl.ds(0, n_dp)]
        return pltpu.make_async_remote_copy(
            src_ref=view, dst_ref=view, send_sem=sib_sems.at[0], recv_sem=sib_sems.at[1],
            device_id={"fsdp": sibling}, device_id_type=MESH,
        )

    sib_wait().wait_recv()

    def gathered(half):
        heads = []
        for m in range(8):
            parts = [orecv[half, m], orecv[half, 8 + m]]
            for g in range(4):
                parts.append(orecv[half, 16 + 4 * g + m // 2, 16 * (m % 2):16 * (m % 2) + 16])
            heads.append(jnp.concatenate(parts, axis=0))
        return jnp.concatenate(heads, axis=1)

    def project(half, c):
        rows = wfull[:, :, half, 2 * q_parts * c:2 * q_parts * (c + 1)].reshape(8 * HD, w_cols)
        return rows

    back_first.wait()
    back_wait(0).wait_recv()
    left = gathered(0)
    for c in range(c_parts):
        acc[:, c * w_cols:(c + 1) * w_cols] = jnp.dot(left, project(0, c), preferred_element_type=F32)
    back_second.wait()
    back_wait(1).wait_recv()
    left = gathered(1)
    for c in range(c_parts):
        columns = slice(c * w_cols, (c + 1) * w_cols)
        mixed = acc[:, columns] + jnp.dot(left, project(1, c), preferred_element_type=F32)
        out_ref[:, columns] = jnp.dot(
            perm[...], mixed.astype(BF16), preferred_element_type=F32
        ).astype(BF16)

    for half in range(2):
        half_wait(half).wait_send()
        back_wait(half).wait_send()
    label_wait().wait_send()
    for k in range(3):
        far_w(k).wait_send()
    for k in range(3):
        near_w(k).wait_send()

    if n_dp == 16:
        view = wfull.at[:, :, :, pl.ds(0, n_dp - 1)]
        pltpu.make_async_remote_copy(
            src_ref=view, dst_ref=view, send_sem=xy_send, recv_sem=xy_recv.at[0],
            device_id={"fsdp": sibling}, device_id_type=MESH,
        ).wait_send()
    sib_wait().wait_send()


def on_device(n_dp, projections, positions, packed_index, clip_length, clip_group, query_gain, key_gain, out_weight):
    q_parts, c_parts = {16: (4, 4), 1: (1, 1)}[n_dp]
    hbm = pl.BlockSpec(memory_space=pltpu.HBM)
    vmem = pl.BlockSpec(memory_space=pltpu.VMEM)
    dma = pltpu.SemaphoreType.DMA
    return pl.pallas_call(
        functools.partial(kernel, n_dp, q_parts, c_parts),
        out_shape=jax.ShapeDtypeStruct((128, 1536), BF16),
        in_specs=[hbm] * 9,
        out_specs=vmem,
        scratch_shapes=[
            pltpu.VMEM((3, 128, 2048), BF16),
            pltpu.VMEM((3, 128), jnp.int32),
            pltpu.VMEM((1, 128), jnp.int32),
            pltpu.SMEM((CLIPS,), jnp.int32),
            pltpu.SMEM((CLIPS,), jnp.int32),
            pltpu.VMEM((1, HD), F32),
            pltpu.VMEM((1, HD), F32),
            pltpu.VMEM((8, HD), F32),
            dma((8,)),
            pltpu.VMEM((2, 32, 3, 32, HD), BF16),
            pltpu.VMEM((2, 32, 3, 32, HD), BF16),
            pltpu.VMEM((GROUPS, 1, HD), F32),
            pltpu.VMEM((32, 1, HD), F32),
            pltpu.VMEM((2, 32, 32, HD), BF16),
            pltpu.VMEM((2, 32, 32, HD), BF16),
            pltpu.VMEM((4, 2, 2, 2 * q_parts * c_parts, 64 // q_parts, 1536 // c_parts), BF16),
            pltpu.VMEM((8 * HD, HD), BF16),
            pltpu.VMEM((8 * HD, HD), BF16),
            pltpu.VMEM((HD, HD), BF16),
            pltpu.VMEM((HD, 1536), F32),
            dma((2,)),
            dma((2,)),
            dma((2,)),
            dma((2,)),
            dma((2,)),
            dma((6,)),
            dma((4, 3)),
            dma,
            dma((n_dp,)),
            dma((2,)),
            pltpu.SemaphoreType.REGULAR((3,)),
            pltpu.SemaphoreType.REGULAR((3,)),
        ],
        compiler_params=pltpu.CompilerParams(
            collective_id=0, has_side_effects=True, vmem_limit_bytes=60 * 1024 * 1024
        ),
        cost_estimate=pl.CostEstimate(flops=3_500_000_000, bytes_accessed=4_000_000, transcendentals=2_500_000),
    )(
        projections.transpose(1, 0, 2),
        positions,
        packed_index.reshape(1, 128),
        clip_length,
        clip_group,
        query_gain.reshape(1, HD),
        key_gain.reshape(1, HD),
        out_weight,
        jnp.asarray(rope_rows()),
    )


def solution(mesh):
    placed = (
        P(("dp", "fsdp"), None, None),
        P(None, ("dp", "fsdp")),
        P(("dp", "fsdp")),
        P("dp"),
        P("dp"),
        P(),
        P(),
        P("fsdp", None),
    )
    return jax.shard_map(
        functools.partial(on_device, mesh.shape["dp"]),
        mesh=mesh, in_specs=placed, out_specs=P(("dp", "fsdp"), None), check_vma=False,
    )
```

```python
import functools
import math

import jax
import jax.numpy as jnp
import numpy as np
from jax import lax
from jax.experimental import pallas as pl
from jax.experimental.pallas import tpu as pltpu
from jax.sharding import PartitionSpec as P

MESH = pl.DeviceIdType.MESH
HD = 128
CLIPS = 24
GROUPS = 6
ROPE_BASE = 256.0
NORM_EPS = 1e-06
MASKED = -30000.0
BF16 = jnp.bfloat16
F32 = jnp.float32


def rope_rows():
    table = np.zeros((8, HD), np.float32)
    lead = HD // 8
    side = (HD - lead) // 2
    offset = 0
    for section in (lead, side, side):
        middle = section // 2
        for column in range(section):
            within = column % middle
            table[0, offset + column] = ROPE_BASE ** (-2.0 * within / section)
            first = column < middle
            table[1, offset + column] = -1.0 if first else 1.0
            table[2, offset + column] = offset + column + (middle if first else -middle)
        offset += section
    return table


def group_base(group):
    return 1024 * group if group < 2 else 2048 + 512 * (group - 2)


def kernel(
    n_dp, q_parts, c_parts,
    x_hbm, pos_hbm, idx_hbm, len_hbm, grp_hbm, qg_hbm, kg_hbm, w_ref, tab_hbm,
    out_ref,
    x_ref, pos_ref, idx_ref, len_ref, grp_ref, qg_ref, kg_ref, tab_ref, in_sems,
    send, recv, lab_send, lab_recv, osend, orecv, wfull, hot_q, hot_k, perm, acc,
    send_sem, recv_sem, lab_sems, ret_send, ret_recv, own_sem,
    wz_sems, xy_send, xy_recv, sib_sems, ring_known, plane_known,
):
    n = 32
    dp = lax.axis_index("dp")
    me = lax.axis_index("fsdp")
    core = me % 2
    chip = me // 2
    sibling = me + 1 - 2 * core
    q_part = dp // c_parts
    c_part = dp % c_parts
    w_rows, w_cols = 64 // q_parts, 1536 // c_parts

    def slot_of(row, side):
        return (row % c_parts) * (2 * q_parts) + side * q_parts + row // c_parts

    def chip_at(away, side):
        return 2 * ((chip + away + 16) % 16) + side

    def near_first(i):
        j = i + 3
        away = jnp.where((j // 2) % 2 == core, j // 4, -(j // 4))
        return jnp.where(i == 0, sibling, chip_at(away, j % 2))

    def far_first(i):
        return near_first(n - 2 - i)

    def tell(semaphore, **place):
        pl.semaphore_signal(semaphore, inc=1, device_id=place, device_id_type=MESH)

    barrier = pltpu.get_barrier_semaphore()

    tell(barrier, fsdp=sibling)
    for away in (1, -1):
        for side in range(2):
            tell(barrier, fsdp=chip_at(away, side))
    if n_dp == 16:
        row, column = dp // 4, dp % 4
        for away in (1, 3):
            tell(barrier, dp=4 * row + (column + away) % 4)
            tell(barrier, dp=4 * ((row + away) % 4) + column)

    arrivals = [
        pltpu.make_async_copy(source, target, in_sems.at[i])
        for i, (source, target) in enumerate((
            (idx_hbm, idx_ref), (len_hbm, len_ref), (grp_hbm, grp_ref), (pos_hbm, pos_ref),
            (qg_hbm, qg_ref), (kg_hbm, kg_ref), (tab_hbm, tab_ref), (x_hbm, x_ref),
        ))
    ]
    for arrival in arrivals:
        arrival.start()
    for arrival in arrivals[:-1]:
        arrival.wait()

    idx = idx_ref[...].astype(F32)
    across = jnp.broadcast_to(idx, (HD, HD))
    down = across.T
    rank = jnp.sum((down < across).astype(F32), axis=0, keepdims=True)
    row_id = lax.broadcasted_iota(jnp.int32, (HD, HD), 0).astype(F32)
    lane_id = lax.broadcasted_iota(jnp.int32, (HD, HD), 1).astype(F32)
    rank_rows = jnp.broadcast_to(rank, (HD, HD))
    to_sorted = (rank_rows == row_id).astype(F32).astype(BF16)
    perm[...] = (rank_rows.T == lane_id).astype(F32).astype(BF16)

    running = [jnp.int32(group_base(g)) for g in range(GROUPS)]
    label = jnp.zeros((1, HD), F32)
    for clip in range(CLIPS):
        length, group = len_ref[clip], grp_ref[clip]
        end = jnp.int32(0)
        for g in range(GROUPS):
            inside = group == g
            running[g] = running[g] + jnp.where(inside, length, 0)
            end = end + jnp.where(inside, running[g], 0)
        label = label + (idx_ref[...] >= end).astype(F32)
    ordered = lax.dot_general(
        jnp.broadcast_to(label, (8, HD)).astype(BF16), to_sorted,
        (((1,), (1,)), ((), ())), preferred_element_type=F32,
    )
    lane = lax.broadcasted_iota(jnp.int32, (8, HD), 1)
    window = 32 * (me % 4)
    for g in range(GROUPS):
        if g < 2:
            shown = pltpu.roll(ordered, (window - 32 * g + HD) % HD, 1)
        else:
            first = 64 + 16 * (g - 2)
            low = pltpu.roll(ordered, (window - first + HD) % HD, 1)
            high = pltpu.roll(ordered, (window + 16 - first + HD) % HD, 1) + 32.0
            shown = jnp.where(lane >= window + 16, high, low)
        shown = jnp.where((lane >= window) & (lane < window + 32), shown, 0.0)
        lab_send[g] = shown[0:1]

    freq = tab_ref[0:1, :]
    sign = tab_ref[1:2, :]
    swap = (jnp.broadcast_to(tab_ref[2:3, :], (HD, HD)) == row_id).astype(F32)
    pos = pos_ref[...].astype(F32)
    section = jnp.where(
        row_id < 16, pos[0:1, :], jnp.where(row_id < 72, pos[1:2, :], pos[2:3, :])
    ).astype(BF16)
    place = lax.dot_general(
        to_sorted, section, (((1,), (1,)), ((), ())), preferred_element_type=F32
    )
    angles = place * freq
    cosine = jnp.cos(angles)
    sine = jnp.sin(angles) * sign
    swap_b = swap.astype(BF16)
    tables = []
    for gain_ref in (qg_ref, kg_ref):
        gain = gain_ref[...]
        gain_down = jnp.broadcast_to(gain, (HD, HD)).T
        turned = jnp.sum(gain_down * swap, axis=0, keepdims=True)
        tables.append((cosine * gain, sine * turned))

    def prepare(half):
        def one(m, carry):
            columns = pl.ds(pl.multiple_of((2 * m + half) * HD, HD), HD)
            for kind in range(3):
                entries = jnp.dot(to_sorted, x_ref[kind, :, columns], preferred_element_type=F32)
                if kind < 2:
                    cos_gain, sin_gain = tables[kind]
                    swapped = jnp.dot(entries.astype(BF16), swap_b, preferred_element_type=F32)
                    mean = jnp.sum(entries * entries, axis=1, keepdims=True) * (1.0 / HD)
                    factor = lax.rsqrt(mean + NORM_EPS)
                    entries = (entries * cos_gain + swapped * sin_gain) * factor
                rows = entries.astype(BF16)
                for g in range(2):
                    send[half, 8 * g + m, kind] = rows[32 * g:32 * g + 32]
                for g in range(4):
                    send[half, 16 + 4 * g + m // 2, kind, pl.ds(pl.multiple_of(16 * (m % 2), 16), 16)] = (
                        rows[64 + 16 * g:80 + 16 * g]
                    )
            return carry

        lax.fori_loop(0, 8, one, 0, unroll=8)

    def send_some(half, first, last, order=far_first):
        @pl.loop(first, last)
        def _(i):
            peer = order(i)
            pltpu.make_async_remote_copy(
                src_ref=send.at[half, peer], dst_ref=recv.at[half, me],
                send_sem=send_sem.at[half], recv_sem=recv_sem.at[half],
                device_id={"fsdp": peer}, device_id_type=MESH,
            ).start()

    def keep_own(half):
        copy = pltpu.make_async_copy(send.at[half, me], recv.at[half, me], own_sem.at[2 + half])
        copy.start()
        return copy

    arrivals[-1].wait()
    prepare(0)
    my_slot = slot_of(dp, core)
    w_own = pltpu.make_async_copy(
        w_ref.at[
            pl.ds(pl.multiple_of(q_part * w_rows, w_rows), w_rows),
            pl.ds(pl.multiple_of(c_part * w_cols, w_cols), w_cols),
        ],
        wfull.at[chip // 4, (chip // 2) % 2, chip % 2, my_slot], own_sem.at[0],
    )
    w_own.start()
    way = 1 - 2 * core

    def far_w(k):
        away = (8, 4, -4)[k] * way
        piece = wfull.at[chip // 4, (chip // 2) % 2, chip % 2, my_slot]
        return pltpu.make_async_remote_copy(
            src_ref=piece, dst_ref=piece, send_sem=wz_sems.at[0, k], recv_sem=wz_sems.at[1, k],
            device_id={"fsdp": chip_at(away, core)}, device_id_type=MESH,
        )

    def near_w(k):
        away = (2, 1, -1)[k] * way
        pieces = wfull.at[:, (chip // 2) % 2, chip % 2, my_slot]
        return pltpu.make_async_remote_copy(
            src_ref=pieces, dst_ref=pieces, send_sem=wz_sems.at[2, k], recv_sem=wz_sems.at[3, k],
            device_id={"fsdp": chip_at(away, core)}, device_id_type=MESH,
        )

    pl.semaphore_wait(barrier, 9 if n_dp == 16 else 5)
    for away in (1, -1):
        tell(ring_known.at[0], fsdp=chip_at(away, core))
    send_some(0, 0, 5, near_first)
    pl.semaphore_wait(ring_known.at[0], 2)
    for away in (2, -2):
        tell(ring_known.at[1], fsdp=chip_at(away, core))
    send_some(0, 5, 9, near_first)
    pl.semaphore_wait(ring_known.at[1], 2)
    for away in (4, -4):
        tell(ring_known.at[2], fsdp=chip_at(away, core))
    w_own.wait()
    far_w(1).start()
    far_w(2).start()
    send_some(0, 9, 17, near_first)
    own_first = keep_own(0)
    if n_dp == 16:
        for away in (1, 3):
            tell(plane_known.at[0], dp=4 * row + (column + away) % 4)
    prepare(1)
    own_second = keep_own(1)
    send_some(1, 0, 9, near_first)
    pl.semaphore_wait(ring_known.at[2], 2)
    far_w(0).start()
    send_some(0, 0, 3)
    if n_dp == 16:
        pl.semaphore_wait(plane_known.at[0], 2)
        for away in (1, 3):
            tell(plane_known.at[1], dp=4 * ((row + away) % 4) + column)
    for k in range(3):
        far_w(k).wait_recv()
    for k in range(3):
        near_w(k).start()
    send_some(0, 3, 14)

    def group_of(peer):
        return jnp.where(peer < 16, peer // 8, 2 + (peer - 16) // 4)

    @pl.loop(0, n - 1)
    def _(i):
        peer = far_first(i)
        pltpu.make_async_remote_copy(
            src_ref=lab_send.at[group_of(peer)], dst_ref=lab_recv.at[me],
            send_sem=lab_sems.at[0], recv_sem=lab_sems.at[1],
            device_id={"fsdp": peer}, device_id_type=MESH,
        ).start()

    lab_own = pltpu.make_async_copy(lab_send.at[group_of(me)], lab_recv.at[me], own_sem.at[1])
    lab_own.start()

    send_some(1, 0, 12)
    for k in range(3):
        near_w(k).wait_recv()

    def xy_copy(to, source):
        part = wfull.at[:, :, :, slot_of(source, core)]
        return pltpu.make_async_remote_copy(
            src_ref=part, dst_ref=part, send_sem=xy_send, recv_sem=xy_recv.at[source],
            device_id={"dp": to}, device_id_type=MESH,
        )

    if n_dp == 16:
        pl.semaphore_wait(plane_known.at[1], 2)
        tell(plane_known.at[2], dp=4 * ((row + 2) % 4) + column)
        pl.semaphore_wait(plane_known.at[2], 1)

        @pl.loop(1, n_dp)
        def _(i):
            xy_copy((dp + i) % n_dp, dp).start()

    def sib_copy(source):
        part = wfull.at[:, :, :, slot_of(source, core)]
        return pltpu.make_async_remote_copy(
            src_ref=part, dst_ref=part, send_sem=sib_sems.at[0], recv_sem=sib_sems.at[1],
            device_id={"fsdp": sibling}, device_id_type=MESH,
        )

    sib_copy(dp).start()
    send_some(1, 12, n - 10)

    def label_wait():
        view = lab_recv.at[pl.ds(0, n - 1)]
        return pltpu.make_async_remote_copy(
            src_ref=view, dst_ref=view, send_sem=lab_sems.at[0], recv_sem=lab_sems.at[1],
            device_id={"fsdp": sibling}, device_id_type=MESH,
        )

    lab_own.wait()
    label_wait().wait_recv()
    for block in range(8):
        row = lab_recv[4 * block] + lab_recv[4 * block + 1] + lab_recv[4 * block + 2] + lab_recv[4 * block + 3]
        same = jnp.broadcast_to(row, (HD, HD)).T == lane_id
        hot_q[block * HD:(block + 1) * HD] = jnp.where(same, 1.0, 0.0).astype(BF16)
        hot_k[block * HD:(block + 1) * HD] = jnp.where(same, 0.0, MASKED).astype(BF16)

    def half_wait(half):
        view = recv.at[half, pl.ds(0, n - 1)]
        return pltpu.make_async_remote_copy(
            src_ref=view, dst_ref=view, send_sem=send_sem.at[half], recv_sem=recv_sem.at[half],
            device_id={"fsdp": sibling}, device_id_type=MESH,
        )

    def back_wait(half):
        view = orecv.at[half, pl.ds(0, n - 1)]
        return pltpu.make_async_remote_copy(
            src_ref=view, dst_ref=view, send_sem=ret_send.at[half], recv_sem=ret_recv.at[half],
            device_id={"fsdp": sibling}, device_id_type=MESH,
        )

    scale = math.log2(math.e) / math.sqrt(HD)

    def attend(half, own_copy):
        own_copy.wait()
        half_wait(half).wait_recv()

        def block(part, carry):
            first = pl.multiple_of(8 * part, 8)
            queries = jnp.concatenate(
                [recv[half, pl.ds(first, 8), 0].reshape(256, HD),
                 hot_q[pl.ds(pl.multiple_of(256 * part, 256), 256)]], axis=1)
            total = jnp.zeros((256, 2 * HD), F32)
            for key_part in range(4):
                keys = jnp.concatenate(
                    [recv[half, 8 * key_part:8 * key_part + 8, 1].reshape(256, HD),
                     hot_k[256 * key_part:256 * key_part + 256]], axis=1)
                values = jnp.concatenate(
                    [recv[half, 8 * key_part:8 * key_part + 8, 2].reshape(256, HD),
                     jnp.ones((256, HD), BF16)], axis=1)
                scores = lax.dot_general(
                    queries, keys, (((1,), (1,)), ((), ())), preferred_element_type=F32)
                weights = jnp.exp2(scores * scale).astype(BF16)
                total = total + jnp.dot(weights, values, preferred_element_type=F32)
            result = (total[:, :HD] / total[:, HD:]).astype(BF16)
            osend[half, pl.ds(first, 8)] = result.reshape(8, 32, HD)

            return carry

        lax.fori_loop(0, 4, block, 0)

        @pl.loop(0, n - 1)
        def _(i):
            peer = far_first(i)
            pltpu.make_async_remote_copy(
                src_ref=osend.at[half, peer], dst_ref=orecv.at[half, me],
                send_sem=ret_send.at[half], recv_sem=ret_recv.at[half],
                device_id={"fsdp": peer}, device_id_type=MESH,
            ).start()

        copy = pltpu.make_async_copy(osend.at[half, me], orecv.at[half, me], own_sem.at[4 + half])
        copy.start()
        return copy

    back_first = attend(0, own_first)

    if n_dp == 16:
        @pl.loop(1, n_dp)
        def _(i):
            source = (dp + n_dp - i) % n_dp
            xy_copy(dp, source).wait_recv()
            sib_copy(source).start()

    back_second = attend(1, own_second)

    def sib_wait():
        view = wfull.at[:, :, :, pl.ds(0, n_dp)]
        return pltpu.make_async_remote_copy(
            src_ref=view, dst_ref=view, send_sem=sib_sems.at[0], recv_sem=sib_sems.at[1],
            device_id={"fsdp": sibling}, device_id_type=MESH,
        )

    sib_wait().wait_recv()

    def gathered(half):
        heads = []
        for m in range(8):
            parts = [orecv[half, m], orecv[half, 8 + m]]
            for g in range(4):
                parts.append(orecv[half, 16 + 4 * g + m // 2, 16 * (m % 2):16 * (m % 2) + 16])
            heads.append(jnp.concatenate(parts, axis=0))
        return jnp.concatenate(heads, axis=1)

    def project(half, c):
        rows = wfull[:, :, half, 2 * q_parts * c:2 * q_parts * (c + 1)].reshape(8 * HD, w_cols)
        return rows

    back_first.wait()
    back_wait(0).wait_recv()
    left = gathered(0)
    for c in range(c_parts):
        acc[:, c * w_cols:(c + 1) * w_cols] = jnp.dot(left, project(0, c), preferred_element_type=F32)
    back_second.wait()
    back_wait(1).wait_recv()
    left = gathered(1)
    for c in range(c_parts):
        columns = slice(c * w_cols, (c + 1) * w_cols)
        mixed = acc[:, columns] + jnp.dot(left, project(1, c), preferred_element_type=F32)
        out_ref[:, columns] = jnp.dot(
            perm[...], mixed.astype(BF16), preferred_element_type=F32
        ).astype(BF16)

    for half in range(2):
        half_wait(half).wait_send()
        back_wait(half).wait_send()
    label_wait().wait_send()
    for k in range(3):
        far_w(k).wait_send()
    for k in range(3):
        near_w(k).wait_send()

    if n_dp == 16:
        view = wfull.at[:, :, :, pl.ds(0, n_dp - 1)]
        pltpu.make_async_remote_copy(
            src_ref=view, dst_ref=view, send_sem=xy_send, recv_sem=xy_recv.at[0],
            device_id={"fsdp": sibling}, device_id_type=MESH,
        ).wait_send()
    sib_wait().wait_send()


def on_device(n_dp, projections, positions, packed_index, clip_length, clip_group, query_gain, key_gain, out_weight):
    q_parts, c_parts = {16: (4, 4), 1: (1, 1)}[n_dp]
    hbm = pl.BlockSpec(memory_space=pltpu.HBM)
    vmem = pl.BlockSpec(memory_space=pltpu.VMEM)
    dma = pltpu.SemaphoreType.DMA
    return pl.pallas_call(
        functools.partial(kernel, n_dp, q_parts, c_parts),
        out_shape=jax.ShapeDtypeStruct((128, 1536), BF16),
        in_specs=[hbm] * 9,
        out_specs=vmem,
        scratch_shapes=[
            pltpu.VMEM((3, 128, 2048), BF16),
            pltpu.VMEM((3, 128), jnp.int32),
            pltpu.VMEM((1, 128), jnp.int32),
            pltpu.SMEM((CLIPS,), jnp.int32),
            pltpu.SMEM((CLIPS,), jnp.int32),
            pltpu.VMEM((1, HD), F32),
            pltpu.VMEM((1, HD), F32),
            pltpu.VMEM((8, HD), F32),
            dma((8,)),
            pltpu.VMEM((2, 32, 3, 32, HD), BF16),
            pltpu.VMEM((2, 32, 3, 32, HD), BF16),
            pltpu.VMEM((GROUPS, 1, HD), F32),
            pltpu.VMEM((32, 1, HD), F32),
            pltpu.VMEM((2, 32, 32, HD), BF16),
            pltpu.VMEM((2, 32, 32, HD), BF16),
            pltpu.VMEM((4, 2, 2, 2 * q_parts * c_parts, 64 // q_parts, 1536 // c_parts), BF16),
            pltpu.VMEM((8 * HD, HD), BF16),
            pltpu.VMEM((8 * HD, HD), BF16),
            pltpu.VMEM((HD, HD), BF16),
            pltpu.VMEM((HD, 1536), F32),
            dma((2,)),
            dma((2,)),
            dma((2,)),
            dma((2,)),
            dma((2,)),
            dma((6,)),
            dma((4, 3)),
            dma,
            dma((n_dp,)),
            dma((2,)),
            pltpu.SemaphoreType.REGULAR((3,)),
            pltpu.SemaphoreType.REGULAR((3,)),
        ],
        compiler_params=pltpu.CompilerParams(
            collective_id=0, has_side_effects=True, vmem_limit_bytes=60 * 1024 * 1024
        ),
        cost_estimate=pl.CostEstimate(flops=3_500_000_000, bytes_accessed=4_000_000, transcendentals=2_500_000),
    )(
        projections.transpose(1, 0, 2),
        positions,
        packed_index.reshape(1, 128),
        clip_length,
        clip_group,
        query_gain.reshape(1, HD),
        key_gain.reshape(1, HD),
        out_weight,
        jnp.asarray(rope_rows()),
    )


def solution(mesh):
    placed = (
        P(("dp", "fsdp"), None, None),
        P(None, ("dp", "fsdp")),
        P(("dp", "fsdp")),
        P("dp"),
        P("dp"),
        P(),
        P(),
        P("fsdp", None),
    )
    return jax.shard_map(
        functools.partial(on_device, mesh.shape["dp"]),
        mesh=mesh, in_specs=placed, out_specs=P(("dp", "fsdp"), None), check_vma=False,
    )
```

```python
import functools
import math

import jax
import jax.numpy as jnp
import numpy as np
from jax import lax
from jax.experimental import pallas as pl
from jax.experimental.pallas import tpu as pltpu
from jax.sharding import PartitionSpec as P

MESH = pl.DeviceIdType.MESH
HD = 128
CLIPS = 24
GROUPS = 6
ROPE_BASE = 256.0
NORM_EPS = 1e-06
MASKED = -30000.0
BF16 = jnp.bfloat16
F32 = jnp.float32


def rope_rows():
    table = np.zeros((8, HD), np.float32)
    lead = HD // 8
    side = (HD - lead) // 2
    offset = 0
    for section in (lead, side, side):
        middle = section // 2
        for column in range(section):
            within = column % middle
            table[0, offset + column] = ROPE_BASE ** (-2.0 * within / section)
            first = column < middle
            table[1, offset + column] = -1.0 if first else 1.0
            table[2, offset + column] = offset + column + (middle if first else -middle)
        offset += section
    return table


def group_base(group):
    return 1024 * group if group < 2 else 2048 + 512 * (group - 2)


def kernel(
    n_dp, q_parts, c_parts,
    x_hbm, pos_hbm, idx_hbm, len_hbm, grp_hbm, qg_hbm, kg_hbm, w_ref, tab_hbm,
    out_hbm,
    out_ref, out_sems, x_ref, pos_ref, idx_ref, len_ref, grp_ref, qg_ref, kg_ref, tab_ref, in_sems,
    send, recv, lab_send, lab_recv, osend, orecv, wfull, hot_q, hot_k, perm, acc,
    send_sem, recv_sem, lab_sems, ret_send, ret_recv, own_sem,
    wz_sems, xy_send, xy_recv, sib_sems, ring_known, plane_known,
):
    n = 32
    dp = lax.axis_index("dp")
    me = lax.axis_index("fsdp")
    core = me % 2
    chip = me // 2
    sibling = me + 1 - 2 * core
    q_part = dp // c_parts
    c_part = dp % c_parts
    w_rows, w_cols = 64 // q_parts, 1536 // c_parts

    def slot_of(row, side):
        return (row % c_parts) * (2 * q_parts) + side * q_parts + row // c_parts

    def chip_at(away, side):
        return 2 * ((chip + away + 16) % 16) + side

    def near_first(i):
        j = i + 3
        away = jnp.where((j // 2) % 2 == core, j // 4, -(j // 4))
        return jnp.where(i == 0, sibling, chip_at(away, j % 2))

    def far_first(i):
        return near_first(n - 2 - i)

    def tell(semaphore, **place):
        pl.semaphore_signal(semaphore, inc=1, device_id=place, device_id_type=MESH)

    barrier = pltpu.get_barrier_semaphore()

    tell(barrier, fsdp=sibling)
    for away in (1, -1):
        for side in range(2):
            tell(barrier, fsdp=chip_at(away, side))
    if n_dp == 16:
        row, column = dp // 4, dp % 4
        for away in (1, 3):
            tell(barrier, dp=4 * row + (column + away) % 4)
            tell(barrier, dp=4 * ((row + away) % 4) + column)

    arrivals = [
        pltpu.make_async_copy(source, target, in_sems.at[i])
        for i, (source, target) in enumerate((
            (idx_hbm, idx_ref), (len_hbm, len_ref), (grp_hbm, grp_ref), (pos_hbm, pos_ref),
            (qg_hbm, qg_ref), (kg_hbm, kg_ref), (tab_hbm, tab_ref), (x_hbm, x_ref),
        ))
    ]
    for arrival in arrivals:
        arrival.start()
    for arrival in arrivals[:-1]:
        arrival.wait()

    idx = idx_ref[...].astype(F32)
    across = jnp.broadcast_to(idx, (HD, HD))
    down = across.T
    rank = jnp.sum((down < across).astype(F32), axis=0, keepdims=True)
    row_id = lax.broadcasted_iota(jnp.int32, (HD, HD), 0).astype(F32)
    lane_id = lax.broadcasted_iota(jnp.int32, (HD, HD), 1).astype(F32)
    rank_rows = jnp.broadcast_to(rank, (HD, HD))
    to_sorted = (rank_rows == row_id).astype(F32).astype(BF16)
    perm[...] = (rank_rows.T == lane_id).astype(F32).astype(BF16)

    running = [jnp.int32(group_base(g)) for g in range(GROUPS)]
    label = jnp.zeros((1, HD), F32)
    for clip in range(CLIPS):
        length, group = len_ref[clip], grp_ref[clip]
        end = jnp.int32(0)
        for g in range(GROUPS):
            inside = group == g
            running[g] = running[g] + jnp.where(inside, length, 0)
            end = end + jnp.where(inside, running[g], 0)
        label = label + (idx_ref[...] >= end).astype(F32)
    ordered = lax.dot_general(
        jnp.broadcast_to(label, (8, HD)).astype(BF16), to_sorted,
        (((1,), (1,)), ((), ())), preferred_element_type=F32,
    )
    lane = lax.broadcasted_iota(jnp.int32, (8, HD), 1)
    window = 32 * (me % 4)
    for g in range(GROUPS):
        if g < 2:
            shown = pltpu.roll(ordered, (window - 32 * g + HD) % HD, 1)
        else:
            first = 64 + 16 * (g - 2)
            low = pltpu.roll(ordered, (window - first + HD) % HD, 1)
            high = pltpu.roll(ordered, (window + 16 - first + HD) % HD, 1) + 32.0
            shown = jnp.where(lane >= window + 16, high, low)
        shown = jnp.where((lane >= window) & (lane < window + 32), shown, 0.0)
        lab_send[g] = shown[0:1]

    freq = tab_ref[0:1, :]
    sign = tab_ref[1:2, :]
    swap = (jnp.broadcast_to(tab_ref[2:3, :], (HD, HD)) == row_id).astype(F32)
    pos = pos_ref[...].astype(F32)
    section = jnp.where(
        row_id < 16, pos[0:1, :], jnp.where(row_id < 72, pos[1:2, :], pos[2:3, :])
    ).astype(BF16)
    place = lax.dot_general(
        to_sorted, section, (((1,), (1,)), ((), ())), preferred_element_type=F32
    )
    angles = place * freq
    cosine = jnp.cos(angles)
    sine = jnp.sin(angles) * sign
    swap_b = swap.astype(BF16)
    tables = []
    for gain_ref in (qg_ref, kg_ref):
        gain = gain_ref[...]
        gain_down = jnp.broadcast_to(gain, (HD, HD)).T
        turned = jnp.sum(gain_down * swap, axis=0, keepdims=True)
        tables.append((cosine * gain, sine * turned))

    def prepare(half):
        def one(m, carry):
            columns = pl.ds(pl.multiple_of((2 * m + half) * HD, HD), HD)
            for kind in range(3):
                entries = jnp.dot(to_sorted, x_ref[kind, :, columns], preferred_element_type=F32)
                if kind < 2:
                    cos_gain, sin_gain = tables[kind]
                    swapped = jnp.dot(entries.astype(BF16), swap_b, preferred_element_type=F32)
                    mean = jnp.sum(entries * entries, axis=1, keepdims=True) * (1.0 / HD)
                    factor = lax.rsqrt(mean + NORM_EPS)
                    entries = (entries * cos_gain + swapped * sin_gain) * factor
                rows = entries.astype(BF16)
                for g in range(2):
                    send[half, 8 * g + m, kind] = rows[32 * g:32 * g + 32]
                for g in range(4):
                    send[half, 16 + 4 * g + m // 2, kind, pl.ds(pl.multiple_of(16 * (m % 2), 16), 16)] = (
                        rows[64 + 16 * g:80 + 16 * g]
                    )
            return carry

        lax.fori_loop(0, 8, one, 0, unroll=8)

    def send_some(half, first, last, order=far_first):
        @pl.loop(first, last)
        def _(i):
            peer = order(i)
            pltpu.make_async_remote_copy(
                src_ref=send.at[half, peer], dst_ref=recv.at[half, me],
                send_sem=send_sem.at[half], recv_sem=recv_sem.at[half],
                device_id={"fsdp": peer}, device_id_type=MESH,
            ).start()

    def keep_own(half):
        copy = pltpu.make_async_copy(send.at[half, me], recv.at[half, me], own_sem.at[2 + half])
        copy.start()
        return copy

    arrivals[-1].wait()
    prepare(0)
    my_slot = slot_of(dp, core)
    w_own = pltpu.make_async_copy(
        w_ref.at[
            pl.ds(pl.multiple_of(q_part * w_rows, w_rows), w_rows),
            pl.ds(pl.multiple_of(c_part * w_cols, w_cols), w_cols),
        ],
        wfull.at[chip // 4, (chip // 2) % 2, chip % 2, my_slot], own_sem.at[0],
    )
    w_own.start()
    way = 1 - 2 * core

    def far_w(k):
        away = (8, 4, -4)[k] * way
        piece = wfull.at[chip // 4, (chip // 2) % 2, chip % 2, my_slot]
        return pltpu.make_async_remote_copy(
            src_ref=piece, dst_ref=piece, send_sem=wz_sems.at[0, k], recv_sem=wz_sems.at[1, k],
            device_id={"fsdp": chip_at(away, core)}, device_id_type=MESH,
        )

    def near_w(k):
        away = (2, 1, -1)[k] * way
        pieces = wfull.at[:, (chip // 2) % 2, chip % 2, my_slot]
        return pltpu.make_async_remote_copy(
            src_ref=pieces, dst_ref=pieces, send_sem=wz_sems.at[2, k], recv_sem=wz_sems.at[3, k],
            device_id={"fsdp": chip_at(away, core)}, device_id_type=MESH,
        )

    pl.semaphore_wait(barrier, 9 if n_dp == 16 else 5)
    for away in (1, -1):
        tell(ring_known.at[0], fsdp=chip_at(away, core))
    send_some(0, 0, 5, near_first)
    pl.semaphore_wait(ring_known.at[0], 2)
    for away in (2, -2):
        tell(ring_known.at[1], fsdp=chip_at(away, core))
    send_some(0, 5, 9, near_first)
    pl.semaphore_wait(ring_known.at[1], 2)
    for away in (4, -4):
        tell(ring_known.at[2], fsdp=chip_at(away, core))
    w_own.wait()
    far_w(1).start()
    far_w(2).start()
    send_some(0, 9, 17, near_first)
    own_first = keep_own(0)
    if n_dp == 16:
        for away in (1, 3):
            tell(plane_known.at[0], dp=4 * row + (column + away) % 4)
    prepare(1)
    own_second = keep_own(1)
    send_some(1, 0, 9, near_first)
    pl.semaphore_wait(ring_known.at[2], 2)
    far_w(0).start()
    send_some(0, 0, 3)
    if n_dp == 16:
        pl.semaphore_wait(plane_known.at[0], 2)
        for away in (1, 3):
            tell(plane_known.at[1], dp=4 * ((row + away) % 4) + column)
    for k in range(3):
        far_w(k).wait_recv()
    for k in range(3):
        near_w(k).start()
    send_some(0, 3, 14)

    def group_of(peer):
        return jnp.where(peer < 16, peer // 8, 2 + (peer - 16) // 4)

    @pl.loop(0, n - 1)
    def _(i):
        peer = far_first(i)
        pltpu.make_async_remote_copy(
            src_ref=lab_send.at[group_of(peer)], dst_ref=lab_recv.at[me],
            send_sem=lab_sems.at[0], recv_sem=lab_sems.at[1],
            device_id={"fsdp": peer}, device_id_type=MESH,
        ).start()

    lab_own = pltpu.make_async_copy(lab_send.at[group_of(me)], lab_recv.at[me], own_sem.at[1])
    lab_own.start()

    send_some(1, 0, 12)
    for k in range(3):
        near_w(k).wait_recv()

    def xy_copy(to, source):
        part = wfull.at[:, :, :, slot_of(source, core)]
        return pltpu.make_async_remote_copy(
            src_ref=part, dst_ref=part, send_sem=xy_send, recv_sem=xy_recv.at[source],
            device_id={"dp": to}, device_id_type=MESH,
        )

    if n_dp == 16:
        pl.semaphore_wait(plane_known.at[1], 2)
        tell(plane_known.at[2], dp=4 * ((row + 2) % 4) + column)
        pl.semaphore_wait(plane_known.at[2], 1)

        @pl.loop(1, n_dp)
        def _(i):
            xy_copy((dp + i) % n_dp, dp).start()

    def sib_copy(source):
        part = wfull.at[:, :, :, slot_of(source, core)]
        return pltpu.make_async_remote_copy(
            src_ref=part, dst_ref=part, send_sem=sib_sems.at[0], recv_sem=sib_sems.at[1],
            device_id={"fsdp": sibling}, device_id_type=MESH,
        )

    sib_copy(dp).start()
    send_some(1, 12, n - 10)

    def label_wait():
        view = lab_recv.at[pl.ds(0, n - 1)]
        return pltpu.make_async_remote_copy(
            src_ref=view, dst_ref=view, send_sem=lab_sems.at[0], recv_sem=lab_sems.at[1],
            device_id={"fsdp": sibling}, device_id_type=MESH,
        )

    lab_own.wait()
    label_wait().wait_recv()
    for block in range(8):
        row = lab_recv[4 * block] + lab_recv[4 * block + 1] + lab_recv[4 * block + 2] + lab_recv[4 * block + 3]
        same = jnp.broadcast_to(row, (HD, HD)).T == lane_id
        hot_q[block * HD:(block + 1) * HD] = jnp.where(same, 1.0, 0.0).astype(BF16)
        hot_k[block * HD:(block + 1) * HD] = jnp.where(same, 0.0, MASKED).astype(BF16)

    def half_wait(half):
        view = recv.at[half, pl.ds(0, n - 1)]
        return pltpu.make_async_remote_copy(
            src_ref=view, dst_ref=view, send_sem=send_sem.at[half], recv_sem=recv_sem.at[half],
            device_id={"fsdp": sibling}, device_id_type=MESH,
        )

    def back_wait(half):
        view = orecv.at[half, pl.ds(0, n - 1)]
        return pltpu.make_async_remote_copy(
            src_ref=view, dst_ref=view, send_sem=ret_send.at[half], recv_sem=ret_recv.at[half],
            device_id={"fsdp": sibling}, device_id_type=MESH,
        )

    scale = math.log2(math.e) / math.sqrt(HD)

    def attend(half, own_copy):
        own_copy.wait()
        half_wait(half).wait_recv()

        def block(part, carry):
            first = pl.multiple_of(8 * part, 8)
            queries = jnp.concatenate(
                [recv[half, pl.ds(first, 8), 0].reshape(256, HD),
                 hot_q[pl.ds(pl.multiple_of(256 * part, 256), 256)]], axis=1)
            total = jnp.zeros((256, 2 * HD), F32)
            for key_part in range(4):
                keys = jnp.concatenate(
                    [recv[half, 8 * key_part:8 * key_part + 8, 1].reshape(256, HD),
                     hot_k[256 * key_part:256 * key_part + 256]], axis=1)
                values = jnp.concatenate(
                    [recv[half, 8 * key_part:8 * key_part + 8, 2].reshape(256, HD),
                     jnp.ones((256, HD), BF16)], axis=1)
                scores = lax.dot_general(
                    queries, keys, (((1,), (1,)), ((), ())), preferred_element_type=F32)
                weights = jnp.exp2(scores * scale).astype(BF16)
                total = total + jnp.dot(weights, values, preferred_element_type=F32)
            result = (total[:, :HD] / total[:, HD:]).astype(BF16)
            osend[half, pl.ds(first, 8)] = result.reshape(8, 32, HD)

            return carry

        lax.fori_loop(0, 4, block, 0)

        @pl.loop(0, n - 1)
        def _(i):
            peer = far_first(i)
            pltpu.make_async_remote_copy(
                src_ref=osend.at[half, peer], dst_ref=orecv.at[half, me],
                send_sem=ret_send.at[half], recv_sem=ret_recv.at[half],
                device_id={"fsdp": peer}, device_id_type=MESH,
            ).start()

        copy = pltpu.make_async_copy(osend.at[half, me], orecv.at[half, me], own_sem.at[4 + half])
        copy.start()
        return copy

    back_first = attend(0, own_first)

    if n_dp == 16:
        @pl.loop(1, n_dp)
        def _(i):
            source = (dp + n_dp - i) % n_dp
            xy_copy(dp, source).wait_recv()
            sib_copy(source).start()

    back_second = attend(1, own_second)

    def sib_wait():
        view = wfull.at[:, :, :, pl.ds(0, n_dp)]
        return pltpu.make_async_remote_copy(
            src_ref=view, dst_ref=view, send_sem=sib_sems.at[0], recv_sem=sib_sems.at[1],
            device_id={"fsdp": sibling}, device_id_type=MESH,
        )

    sib_wait().wait_recv()

    def gathered(half):
        heads = []
        for m in range(8):
            parts = [orecv[half, m], orecv[half, 8 + m]]
            for g in range(4):
                parts.append(orecv[half, 16 + 4 * g + m // 2, 16 * (m % 2):16 * (m % 2) + 16])
            heads.append(jnp.concatenate(parts, axis=0))
        return jnp.concatenate(heads, axis=1)

    def project(half, c):
        rows = wfull[:, :, half, 2 * q_parts * c:2 * q_parts * (c + 1)].reshape(8 * HD, w_cols)
        return rows

    back_first.wait()
    back_wait(0).wait_recv()
    left = gathered(0)
    for c in range(c_parts):
        acc[:, c * w_cols:(c + 1) * w_cols] = jnp.dot(left, project(0, c), preferred_element_type=F32)
    back_second.wait()
    back_wait(1).wait_recv()
    left = gathered(1)
    for c in range(c_parts):
        columns = slice(c * w_cols, (c + 1) * w_cols)
        mixed = acc[:, columns] + jnp.dot(left, project(1, c), preferred_element_type=F32)
        out_ref[:, columns] = jnp.dot(
            perm[...], mixed.astype(BF16), preferred_element_type=F32
        ).astype(BF16)
        pltpu.make_async_copy(out_ref.at[:, columns], out_hbm.at[:, columns], out_sems.at[c]).start()

    for half in range(2):
        half_wait(half).wait_send()
        back_wait(half).wait_send()
    label_wait().wait_send()
    for k in range(3):
        far_w(k).wait_send()
    for k in range(3):
        near_w(k).wait_send()

    if n_dp == 16:
        view = wfull.at[:, :, :, pl.ds(0, n_dp - 1)]
        pltpu.make_async_remote_copy(
            src_ref=view, dst_ref=view, send_sem=xy_send, recv_sem=xy_recv.at[0],
            device_id={"fsdp": sibling}, device_id_type=MESH,
        ).wait_send()
    sib_wait().wait_send()
    for c in range(c_parts):
        columns = slice(c * w_cols, (c + 1) * w_cols)
        pltpu.make_async_copy(out_ref.at[:, columns], out_hbm.at[:, columns], out_sems.at[c]).wait()


def on_device(n_dp, projections, positions, packed_index, clip_length, clip_group, query_gain, key_gain, out_weight):
    q_parts, c_parts = {16: (4, 4), 1: (1, 1)}[n_dp]
    hbm = pl.BlockSpec(memory_space=pltpu.HBM)
    dma = pltpu.SemaphoreType.DMA
    return pl.pallas_call(
        functools.partial(kernel, n_dp, q_parts, c_parts),
        out_shape=jax.ShapeDtypeStruct((128, 1536), BF16),
        in_specs=[hbm] * 9,
        out_specs=hbm,
        scratch_shapes=[
            pltpu.VMEM((128, 1536), BF16),
            dma((c_parts,)),
            pltpu.VMEM((3, 128, 2048), BF16),
            pltpu.VMEM((3, 128), jnp.int32),
            pltpu.VMEM((1, 128), jnp.int32),
            pltpu.SMEM((CLIPS,), jnp.int32),
            pltpu.SMEM((CLIPS,), jnp.int32),
            pltpu.VMEM((1, HD), F32),
            pltpu.VMEM((1, HD), F32),
            pltpu.VMEM((8, HD), F32),
            dma((8,)),
            pltpu.VMEM((2, 32, 3, 32, HD), BF16),
            pltpu.VMEM((2, 32, 3, 32, HD), BF16),
            pltpu.VMEM((GROUPS, 1, HD), F32),
            pltpu.VMEM((32, 1, HD), F32),
            pltpu.VMEM((2, 32, 32, HD), BF16),
            pltpu.VMEM((2, 32, 32, HD), BF16),
            pltpu.VMEM((4, 2, 2, 2 * q_parts * c_parts, 64 // q_parts, 1536 // c_parts), BF16),
            pltpu.VMEM((8 * HD, HD), BF16),
            pltpu.VMEM((8 * HD, HD), BF16),
            pltpu.VMEM((HD, HD), BF16),
            pltpu.VMEM((HD, 1536), F32),
            dma((2,)),
            dma((2,)),
            dma((2,)),
            dma((2,)),
            dma((2,)),
            dma((6,)),
            dma((4, 3)),
            dma,
            dma((n_dp,)),
            dma((2,)),
            pltpu.SemaphoreType.REGULAR((3,)),
            pltpu.SemaphoreType.REGULAR((3,)),
        ],
        compiler_params=pltpu.CompilerParams(
            collective_id=0, has_side_effects=True, vmem_limit_bytes=60 * 1024 * 1024
        ),
        cost_estimate=pl.CostEstimate(flops=3_500_000_000, bytes_accessed=4_000_000, transcendentals=2_500_000),
    )(
        projections.transpose(1, 0, 2),
        positions,
        packed_index.reshape(1, 128),
        clip_length,
        clip_group,
        query_gain.reshape(1, HD),
        key_gain.reshape(1, HD),
        out_weight,
        jnp.asarray(rope_rows()),
    )


def solution(mesh):
    placed = (
        P(("dp", "fsdp"), None, None),
        P(None, ("dp", "fsdp")),
        P(("dp", "fsdp")),
        P("dp"),
        P("dp"),
        P(),
        P(),
        P("fsdp", None),
    )
    return jax.shard_map(
        functools.partial(on_device, mesh.shape["dp"]),
        mesh=mesh, in_specs=placed, out_specs=P(("dp", "fsdp"), None), check_vma=False,
    )
```
